32 devices in a mesh: grp: 2 (over y), ctx: 4 (over z), head: 4 (over x, core).
Axes of the slice: x: 2, y: 2, z: 4, core: 2. Of those that a mesh axis runs over, the one named last changes fastest.
Arguments:
- query_raw: bfloat16 [2048, 2048], P(('grp', 'ctx'), 'head'), parts along dimension 0, may hold values from -6 to 6
- key_raw: bfloat16 [2048, 2048], P(('grp', 'ctx'), 'head'), parts along dimension 0, may hold values from -6 to 6
- value_raw: bfloat16 [2048, 4096], P(('grp', 'ctx'), 'head'), parts along dimension 0, may hold values from -6 to 6
- out_gate: bfloat16 [2048, 4096], P(('grp', 'ctx'), 'head'), parts along dimension 0, may hold values from -6 to 6
- conv_query: float32 [4, 2048], P(None, 'head'), may hold values from -3 to 3
- conv_key: float32 [4, 2048], P(None, 'head'), may hold values from -3 to 3
- conv_value: float32 [4, 4096], P(None, 'head'), may hold values from -3 to 3
- decay_log: float32 [2048, 32], P(('grp', 'ctx'), 'head'), parts along dimension 0, may hold values from -1.6 to 0
- write_beta: float32 [2048, 32], P(('grp', 'ctx'), 'head'), parts along dimension 0, may hold values from 0.02 to 0.9
- norm_gain: float32 [128], replicated, may hold values from 0.5 to 1.5
- query_heads: bfloat16 [2048, 4096], P(('grp', 'ctx'), 'head'), parts along dimension 0, may hold values from -7 to 7
- gate_heads: bfloat16 [2048, 4096], P(('grp', 'ctx'), 'head'), parts along dimension 0, may hold values from -6 to 6
- key_heads: bfloat16 [2048, 512], P(('grp', 'ctx')), parts along dimension 0, may hold values from -7 to 7
- value_heads: bfloat16 [2048, 512], P(('grp', 'ctx')), parts along dimension 0, may hold values from -6 to 6
- query_gain: float32 [256], replicated, may hold values from 0.7 to 4.5
- key_gain: float32 [256], replicated, may hold values from 0.7 to 4.5
Outputs:
- deltanet_out: bfloat16 [2048, 4096], P(('grp', 'ctx'), 'head'), parts along dimension 0
- attention_out: bfloat16 [2048, 4096], P(('grp', 'ctx'), 'head'), parts along dimension 0
The draws below stay inside these ranges and needn't reach their ends.
There are 2 independent parts, one for each index of `grp`. The reference program is written for one: setup_inputs(seed, part) draws one part's arguments, and reference() takes and returns one part's arrays. A program takes and returns all parts, laid end to end along the dimension named above; an argument that names none is the same for every part. Nothing has to cross between parts.
All inputs are finite; a program needn't handle non-finite values.
Results may differ from the reference program's by a relative error of at most 0.01.
The reference program's roundings to bfloat16 on the way count: a program that leaves them out, or rounds other values in their place, can miss the bound.
Values may be sent and summed in bfloat16 or wider, within the bound.
A program may use at most 128 MiB of HBM per device.

```python
import math
import jax
import jax.numpy as jnp
from jax import lax

D_K = 128
D_V = 128
K_HEADS = 16
VALUE_HEAD_COUNT = 32
CONV = 4
SPAN = 64
Q_HEADS = 16
KV_HEADS = 2
HEAD_DIM = 256
TOK_DEV = 256
WINDOW_TOKENS = 1024


def gate_law(key):
    parallel_flows = jax.random.split(jax.random.fold_in(key, 101), 9)
    slow_share = 0.75
    slow_heads = jax.random.uniform(parallel_flows[0], (VALUE_HEAD_COUNT,)) < slow_share
    slow_rate = jnp.exp(jax.random.uniform(parallel_flows[1], (VALUE_HEAD_COUNT,), jnp.float32, math.log(2e-05), math.log(5e-05)))
    fast_rate = jnp.exp(jax.random.uniform(parallel_flows[2], (VALUE_HEAD_COUNT,), jnp.float32, math.log(0.02), math.log(0.035)))
    baseline_rate = jnp.where(slow_heads, slow_rate, fast_rate)
    block_count = WINDOW_TOKENS // TOK_DEV
    block_factor = jnp.exp(jax.random.uniform(parallel_flows[3], (block_count, VALUE_HEAD_COUNT), jnp.float32, math.log(0.5), math.log(2.0)))
    each_row_value = jnp.repeat(block_factor, TOK_DEV, axis=0)
    random_perturbation = jnp.exp(jax.random.uniform(parallel_flows[4], (WINDOW_TOKENS, VALUE_HEAD_COUNT), jnp.float32, math.log(0.6), math.log(1.6)))
    spike_rows = jax.random.randint(parallel_flows[5], (2,), 0, WINDOW_TOKENS)
    spike_penalty = jax.random.uniform(parallel_flows[6], (2, VALUE_HEAD_COUNT), jnp.float32, 0.2, 0.5)
    row_position_index = jnp.arange(WINDOW_TOKENS)
    spike_events = jnp.zeros((WINDOW_TOKENS, VALUE_HEAD_COUNT), jnp.float32)
    for spike_index in range(2):
        spike_events = spike_events + jnp.where(row_position_index[:, None] == spike_rows[spike_index], -jnp.log(1.0 - spike_penalty[spike_index])[None, :], 0.0)
    decay_factor = -(baseline_rate[None, :] * each_row_value * random_perturbation) - spike_events
    slow_beta = jnp.exp(jax.random.uniform(parallel_flows[7], (WINDOW_TOKENS, VALUE_HEAD_COUNT), jnp.float32, math.log(0.02), math.log(0.05)))
    fast_beta = jnp.exp(jax.random.uniform(parallel_flows[8], (WINDOW_TOKENS, VALUE_HEAD_COUNT), jnp.float32, math.log(0.05), math.log(0.9)))
    beta = jnp.where(slow_heads[None, :], slow_beta, fast_beta)
    return (decay_factor, beta)


def draw_decay_log(key, part):
    return gate_law(key)[0]


def draw_write_beta(key, part):
    return gate_law(key)[1]


def attention_law(key):
    stream = jax.random.fold_in(key, 301)
    key_part = jax.random.truncated_normal(jax.random.fold_in(stream, 1), -6.0, 6.0, (WINDOW_TOKENS, KV_HEADS * HEAD_DIM), jnp.float32)
    query_part = jax.random.truncated_normal(jax.random.fold_in(stream, 2), -6.0, 6.0, (WINDOW_TOKENS, Q_HEADS * HEAD_DIM), jnp.float32)
    return (key_part, query_part)


def draw_key_heads(key, part):
    return attention_law(key)[0].astype(jnp.bfloat16)


def draw_query_heads(key, part):
    return attention_law(key)[1].astype(jnp.bfloat16)


def draw_query_gain(key, part):
    stream = jax.random.fold_in(key, 401)
    return jax.random.uniform(stream, (HEAD_DIM,), jnp.float32, 0.7, 1.3)


def draw_key_gain(key, part):
    stream = jax.random.fold_in(key, 402)
    return jax.random.uniform(stream, (HEAD_DIM,), jnp.float32, 0.7, 1.3)


def block_scale(stream_key, extent, cuts, least, top_value):
    loudness = 1.0
    for axis_at, parts in cuts:
        draws = jax.random.uniform(jax.random.fold_in(jax.random.fold_in(stream_key, 6), axis_at), (parts,), jnp.float32, least / len(cuts), top_value / len(cuts))
        loudness = loudness * jnp.repeat(jnp.exp(draws), extent[axis_at] // parts).reshape((-1,) + (1,) * (len(extent) - 1 - axis_at))
    return loudness


def centred(rng, dims, spread, reach, shards=(), held_as=jnp.bfloat16):
    entries = jax.random.normal(rng, dims, jnp.float32) * spread
    if len(shards) > 0:
        entries = block_scale(rng, dims, shards, -0.22, 0.18) * entries
    return jnp.clip(entries, min=-reach, max=reach).astype(held_as)


def setup_inputs(seed: int = 0, part: int = 0) -> dict:
    keys = jax.random.split(jax.random.key(seed), 17)
    part_keys = jax.random.split(jax.random.fold_in(keys[16], part), 17)
    return {
        "query_raw": centred(part_keys[0], (WINDOW_TOKENS, K_HEADS * D_K), 1.0, 6.0, ((0, 4), (1, 4))),
        "key_raw": centred(part_keys[1], (WINDOW_TOKENS, K_HEADS * D_K), 1.0, 6.0, ((0, 4), (1, 4))),
        "value_raw": centred(part_keys[2], (WINDOW_TOKENS, VALUE_HEAD_COUNT * D_V), 1.0, 6.0, ((0, 4), (1, 4))),
        "out_gate": centred(part_keys[3], (WINDOW_TOKENS, VALUE_HEAD_COUNT * D_V), 1.0, 6.0, ((0, 4), (1, 4))),
        "conv_query": centred(keys[4], (CONV, K_HEADS * D_K), CONV ** -0.5, 3.0, ((1, 4),), jnp.float32),
        "conv_key": centred(keys[5], (CONV, K_HEADS * D_K), CONV ** -0.5, 3.0, ((1, 4),), jnp.float32),
        "conv_value": centred(keys[6], (CONV, VALUE_HEAD_COUNT * D_V), CONV ** -0.5, 3.0, ((1, 4),), jnp.float32),
        "decay_log": draw_decay_log(jax.random.fold_in(jax.random.fold_in(keys[16], part), 71), part),
        "write_beta": draw_write_beta(jax.random.fold_in(jax.random.fold_in(keys[16], part), 71), part),
        "norm_gain": jnp.clip(1.0 + 0.1 * jax.random.normal(keys[9], (D_V,), jnp.float32), 0.5, 1.5),
        "query_heads": draw_query_heads(jax.random.fold_in(jax.random.fold_in(keys[16], part), 71), part),
        "gate_heads": centred(part_keys[11], (WINDOW_TOKENS, Q_HEADS * HEAD_DIM), 1.0, 6.0, ((0, 4), (1, 4))),
        "key_heads": draw_key_heads(jax.random.fold_in(jax.random.fold_in(keys[16], part), 71), part),
        "value_heads": centred(part_keys[13], (WINDOW_TOKENS, KV_HEADS * HEAD_DIM), 1.0, 6.0, ((0, 4),)),
        "query_gain": draw_query_gain(jax.random.fold_in(keys[16], 71), part),
        "key_gain": draw_key_gain(jax.random.fold_in(keys[16], 71), part),
    }


HIGHEST = lax.Precision.HIGHEST
ROPE_THETA = 10000000.0

def matmul_heads(left, right):
    return jnp.einsum('hij,hjk->hik', left, right, precision=HIGHEST)

def unit_lower_inverse(strict_part):
    length = strict_part.shape[-1]
    identity = jnp.eye(length, dtype=jnp.float32)
    power_term = -strict_part
    inverse = identity + power_term
    for level in range(1, max(1, (length - 1).bit_length())):
        power_term = matmul_heads(power_term, power_term)
        inverse = matmul_heads(inverse, identity + power_term)
    return inverse

def delta_span(memory, queries, keys_in, values_in, decay_part, beta_part, with_output):
    length = keys_in.shape[1]
    cumulative = jnp.cumsum(decay_part, axis=1)
    lower_incl = jnp.tril(jnp.ones((length, length), dtype=bool))
    strict_mask = jnp.tril(jnp.ones((length, length), dtype=jnp.float32), -1)
    spacing = jnp.where(lower_incl, cumulative[:, :, None] - cumulative[:, None, :], 0.0)
    within = jnp.where(lower_incl, jnp.exp(spacing), 0.0)
    key_gram = matmul_heads(keys_in, jnp.swapaxes(keys_in, 1, 2))
    coupling = beta_part[:, :, None] * key_gram * within * strict_mask
    inverse = unit_lower_inverse(coupling)
    decay_now = jnp.exp(cumulative)
    weights_left = matmul_heads(inverse, (beta_part * decay_now)[:, :, None] * keys_in)
    targets = matmul_heads(inverse, beta_part[:, :, None] * values_in)
    fresh = targets - matmul_heads(weights_left, memory)
    last_sum = cumulative[:, -1]
    scaled_keys = keys_in * jnp.exp(last_sum[:, None] - cumulative)[:, :, None]
    carried = jnp.exp(last_sum)[:, None, None] * memory + matmul_heads(jnp.swapaxes(scaled_keys, 1, 2), fresh)
    if with_output:
        inner = matmul_heads(queries, jnp.swapaxes(keys_in, 1, 2)) * within
        output = matmul_heads(queries * decay_now[:, :, None], memory) + matmul_heads(inner, fresh)
        return (carried, output)
    return (carried, None)

def run_spans(memory, queries, keys_in, values_in, decay_log, write_beta, with_output):
    row_count = keys_in.shape[0]
    span_count = row_count // SPAN

    def shaped(array):
        return array.reshape((span_count, SPAN) + array.shape[1:])

    def advance(memory_in, pieces):
        span_query, span_key, span_value, span_decay, span_beta = pieces
        return delta_span(memory_in, jnp.swapaxes(span_query, 0, 1), jnp.swapaxes(span_key, 0, 1), jnp.swapaxes(span_value, 0, 1), span_decay.T, span_beta.T, with_output)
    final, outputs = lax.scan(advance, memory, (shaped(queries), shaped(keys_in), shaped(values_in), shaped(decay_log), shaped(write_beta)))
    if with_output:
        outputs = jnp.swapaxes(outputs, 1, 2).reshape(row_count, outputs.shape[1], outputs.shape[3])
    return (final, outputs)

def conv_silu(rim_block, local_block, kernel):
    taps = kernel.shape[0]
    length = local_block.shape[0]
    padded = jnp.concatenate([rim_block, local_block], 0).astype(jnp.float32)
    summed = kernel[0] * padded[0:length]
    for tap_index in range(1, taps):
        summed = summed + kernel[tap_index] * padded[tap_index:tap_index + length]
    return jax.nn.silu(summed)

def unit_rows(matrix):
    return matrix * lax.rsqrt(lax.optimization_barrier(jnp.sum(matrix * matrix, -1, keepdims=True)) + 1e-06)

def delta_inputs(query_conv, key_conv, value_conv):
    row_count = query_conv.shape[0]
    repeats = VALUE_HEAD_COUNT // K_HEADS
    queries = unit_rows(query_conv.reshape(row_count, -1, D_K)) * D_K ** (-0.5)
    keys_in = unit_rows(key_conv.reshape(row_count, -1, D_K))
    queries = jnp.repeat(queries, repeats, axis=1)
    keys_in = jnp.repeat(keys_in, repeats, axis=1)
    values_in = value_conv.reshape(row_count, -1, D_V)
    return (queries, keys_in, values_in)

def gated_norm(output, gate_raw, gain):
    normed = output * lax.rsqrt(lax.optimization_barrier(jnp.mean(output * output, -1, keepdims=True)) + 1e-06) * gain
    gated = normed.reshape(gate_raw.shape) * jax.nn.silu(gate_raw.astype(jnp.float32))
    return gated.astype(jnp.bfloat16)

def rope_norm(heads_in, gain, positions):
    normed = heads_in * lax.rsqrt(lax.optimization_barrier(jnp.mean(heads_in * heads_in, -1, keepdims=True)) + 1e-06) * gain
    half_width = heads_in.shape[-1] // 8
    frequency = ROPE_THETA ** (-jnp.arange(half_width, dtype=jnp.float32) / half_width)
    angles = positions.astype(jnp.float32)[:, None] * frequency[None, :]
    cosine = jnp.cos(angles)[:, None, :]
    sine = jnp.sin(angles)[:, None, :]
    first_part = normed[..., :half_width]
    second_part = normed[..., half_width:2 * half_width]
    rotated = jnp.concatenate([first_part * cosine - second_part * sine, second_part * cosine + first_part * sine, normed[..., 2 * half_width:]], -1)
    return rotated.astype(jnp.bfloat16)

def reference(query_raw, key_raw, value_raw, out_gate, conv_query, conv_key, conv_value, decay_log, write_beta, norm_gain, query_heads, gate_heads, key_heads, value_heads, query_gain, key_gain):
    tokens = query_raw.shape[0]
    rim_count = CONV - 1
    query_conv = conv_silu(jnp.zeros((rim_count, query_raw.shape[1]), jnp.bfloat16), query_raw, conv_query)
    key_conv = conv_silu(jnp.zeros((rim_count, key_raw.shape[1]), jnp.bfloat16), key_raw, conv_key)
    value_conv = conv_silu(jnp.zeros((rim_count, value_raw.shape[1]), jnp.bfloat16), value_raw, conv_value)
    queries, keys_in, values_in = delta_inputs(query_conv, key_conv, value_conv)
    memory = jnp.zeros((VALUE_HEAD_COUNT, D_K, D_V), jnp.float32)
    unused, delta_out = run_spans(memory, queries, keys_in, values_in, decay_log, write_beta, True)
    deltanet_out = gated_norm(delta_out, out_gate, norm_gain)
    positions = jnp.arange(tokens, dtype=jnp.int32)
    query_rot = rope_norm(query_heads.astype(jnp.float32).reshape(tokens, Q_HEADS, HEAD_DIM), query_gain, positions)
    key_rot = rope_norm(key_heads.astype(jnp.float32).reshape(tokens, KV_HEADS, HEAD_DIM), key_gain, positions)
    value_all = value_heads.reshape(tokens, KV_HEADS, HEAD_DIM)
    block_rows = 4 * TOK_DEV
    group_size = Q_HEADS // KV_HEADS
    score_scale = HEAD_DIM ** (-0.5)

    def one_head(head_index):
        kv_index = head_index // group_size
        head_keys = lax.dynamic_index_in_dim(key_rot, kv_index, 1, False)
        head_values = lax.dynamic_index_in_dim(value_all, kv_index, 1, False)
        head_queries = lax.dynamic_index_in_dim(query_rot, head_index, 1, False)

        def one_block(first_row):
            block_queries = lax.dynamic_slice_in_dim(head_queries, first_row, block_rows, 0)
            scores = jnp.dot(block_queries, head_keys.T, preferred_element_type=jnp.float32) * score_scale
            query_pos = first_row + jnp.arange(block_rows, dtype=jnp.int32)
            allowed = positions[None, :] <= query_pos[:, None]
            masked = jnp.where(allowed, scores, -1e+30)
            largest = lax.optimization_barrier(jnp.max(masked, -1, keepdims=True))
            expos = jnp.where(allowed, jnp.exp(masked - largest), 0.0)
            totals = lax.optimization_barrier(jnp.sum(expos, -1, keepdims=True))
            mixed_sum = jnp.dot(expos.astype(jnp.bfloat16), head_values, preferred_element_type=jnp.float32)
            return mixed_sum / totals
        starts = jnp.arange(tokens // block_rows, dtype=jnp.int32) * block_rows
        return lax.map(one_block, starts).reshape(tokens, HEAD_DIM)
    heads_out = lax.map(one_head, jnp.arange(Q_HEADS, dtype=jnp.int32))
    gated = jnp.swapaxes(heads_out, 0, 1).reshape(tokens, Q_HEADS * HEAD_DIM) * jax.nn.sigmoid(gate_heads.astype(jnp.float32))
    return (deltanet_out, gated.astype(jnp.bfloat16))
```

```python
import functools

import jax
import jax.numpy as jnp
import numpy as np
from jax import lax
from jax.experimental import pallas as pl
from jax.experimental.pallas import tpu as pltpu
from jax.sharding import PartitionSpec as P

D_K = 128
D_V = 128
K_HEADS = 16
VALUE_HEAD_COUNT = 32
CONV = 4
Q_HEADS = 16
KV_HEADS = 2
HEAD_DIM = 256
ROPE_THETA = 10000000.0
REPEATS = VALUE_HEAD_COUNT // K_HEADS
RIM = 16

HIGHEST = lax.Precision.HIGHEST
MESH = pl.DeviceIdType.MESH
F32 = jnp.float32
BF16 = jnp.bfloat16


def mm(left, right):
    return jnp.dot(left.astype(BF16), right.astype(BF16), preferred_element_type=F32)


def mmt(left, right):
    return lax.dot_general(
        left.astype(BF16),
        right.astype(BF16),
        (((1,), (1,)), ((), ())),
        preferred_element_type=F32,
    )


def sigmoid(x):
    return 1.0 / (1.0 + jnp.exp(-x))


def unit_rows(x):
    return x * lax.rsqrt(jnp.sum(x * x, -1, keepdims=True) + 1e-06)


def iotas(rows):
    row = lax.broadcasted_iota(jnp.int32, (rows, rows), 0)
    col = lax.broadcasted_iota(jnp.int32, (rows, rows), 1)
    return row, col


def delta_local(gram, scores, key, key_t, query, value, cum, cum_row, beta):
    rows = gram.shape[0]
    row, col = iotas(rows)
    lower = row >= col
    within = jnp.where(lower, jnp.exp(jnp.where(lower, cum - cum_row, 0.0)), 0.0)
    coupling = jnp.where(row > col, beta * gram * within, 0.0).astype(BF16)
    zero = jnp.zeros_like(coupling)
    same16 = (row // 16) == (col // 16)
    same64 = (row // 64) == (col // 64)

    power = jnp.where(same16, -coupling, zero)
    extra = power.astype(F32)
    for _ in range(3):
        power = mm(power, power).astype(BF16)
        extra = extra + power.astype(F32) + mm(extra, power)

    rest = jnp.where(same64 & ~same16, coupling, zero)
    step = -(rest.astype(F32) + mm(extra, rest))
    step2 = mm(step, step)
    grow = step + step2 + mm(step, step2)
    extra = extra + grow + mm(grow, extra)

    rest = jnp.where(same64, zero, coupling)
    step = (-(rest.astype(F32) + mm(extra, rest))).astype(BF16)
    step2 = mm(step, step)
    decay_now = jnp.exp(cum)
    right = jnp.concatenate([beta * value, (beta * decay_now) * key], -1)
    solved = right + mm(extra, right)
    solved = solved + mm(step2, solved)
    solved = (solved + mm(step, solved)).astype(BF16)

    inner = (scores * within).astype(BF16)
    both = mm(inner, solved)
    out_local = both[:, :D_V]
    state_query = query * decay_now - both[:, D_V:]
    last = cum[rows - 1 :, :]
    ended = mm(key_t * jnp.exp(last - cum_row), solved)
    offset = ended[:, :D_V]
    krow, kcol = iotas(D_K)
    transfer = jnp.where(krow == kcol, jnp.exp(last), 0.0) - ended[:, D_V:]
    return out_local, state_query, offset, transfer


def rope_norm(x, gain, cosine, sine):
    normed = x * lax.rsqrt(jnp.mean(x * x, -1, keepdims=True) + 1e-06) * gain
    half = HEAD_DIM // 8
    front = normed[:, :128]
    lane = lax.broadcasted_iota(jnp.int32, front.shape, 1)
    partner = jnp.where(lane < half, pltpu.roll(front, 128 - half, 1), pltpu.roll(front, half, 1))
    front = front * cosine + partner * sine
    return jnp.concatenate([front, normed[:, 128:]], -1).astype(BF16)


def kernel(n, *refs):
    ins = refs[:18]
    (
        qraw_h, kraw_h, vraw_h, ogate_h, cq_h, ck_h, cv_h, decay_h, beta_h, ngain_h,
        qh_h, gh_h, kh_h, vh_h, qgain_h, kgain_h, cos_h, sin_h,
    ) = ins
    dn_out, at_out = refs[18:20]
    (
        qraw, kraw, vraw, ogate, cq, ck, cv, decay, beta_in, ngain,
        qh, gh, kh, qgain, kgain, cosine, sine,
        rim_q, rim_k, rim_v, pad, cum_s, cumt_s,
        out_local_s, state_query_s, offset_s, transfer_s,
        kbuf, vbuf, qrot, m_s, l_s, acc_s, in_buf, send_buf, dn_v, at_v,
        load_sem, rim_send, rim_recv, kv_send, kv_recv, st_send, st_recv, out_sem,
    ) = refs[20:]
    rows = qraw.shape[0]
    me = lax.axis_index("ctx")
    head = lax.axis_index("head")
    later = jnp.minimum(me + 1, n - 1)
    behind = jnp.maximum(me - 1, 0)
    key_heads = qraw.shape[1] // D_K
    value_heads = vraw.shape[1] // D_V
    q_heads = qh.shape[1] // HEAD_DIM
    kv_index = head * q_heads // (Q_HEADS // KV_HEADS)
    kv_cols = pl.ds(pl.multiple_of(kv_index * HEAD_DIM, HEAD_DIM), HEAD_DIM)
    own_rows = pl.ds(pl.multiple_of(me * rows, rows), rows)

    barrier = pltpu.get_barrier_semaphore()

    @pl.loop(1, n)
    def _(d):
        pl.semaphore_signal(
            barrier, inc=1, device_id={"ctx": lax.rem(me + d, n)}, device_id_type=MESH
        )

    pairs = [
        (kh_h.at[:, kv_cols], kh),
        (cos_h.at[own_rows], cosine),
        (sin_h.at[own_rows], sine),
        (kgain_h, kgain),
        (vh_h.at[:, kv_cols], vbuf.at[me]),
        (qraw_h, qraw),
        (kraw_h, kraw),
        (vraw_h, vraw),
        (decay_h, decay),
        (beta_h, beta_in),
        (cq_h, cq),
        (ck_h, ck),
        (cv_h, cv),
        (ngain_h, ngain),
        (qgain_h, qgain),
        (qh_h, qh),
        (gh_h, gh),
        (ogate_h, ogate),
    ]
    loads = [
        pltpu.make_async_copy(source, target, load_sem.at[i])
        for i, (source, target) in enumerate(pairs)
    ]
    for load in loads:
        load.start()

    for load in loads[:5]:
        load.wait()
    kbuf[me] = rope_norm(kh[...].astype(F32), kgain[...], cosine[...], sine[...])
    for load in loads[5:15]:
        load.wait()
    pl.semaphore_wait(barrier, n - 1)

    def rim_copy(raw, rim, i, dest):
        return pltpu.make_async_remote_copy(
            src_ref=raw.at[pl.ds(rows - RIM, RIM)],
            dst_ref=rim,
            send_sem=rim_send.at[i],
            recv_sem=rim_recv.at[i],
            device_id={"ctx": dest},
            device_id_type=MESH,
        )

    def kv_copy(buf, i, block, dest):
        return pltpu.make_async_remote_copy(
            src_ref=buf.at[block],
            dst_ref=buf.at[block],
            send_sem=kv_send.at[i, dest],
            recv_sem=kv_recv.at[i, block],
            device_id={"ctx": dest},
            device_id_type=MESH,
        )

    def state_copy(h, dest):
        return pltpu.make_async_remote_copy(
            src_ref=send_buf.at[h],
            dst_ref=in_buf.at[h],
            send_sem=st_send.at[h],
            recv_sem=st_recv.at[h],
            device_id={"ctx": dest},
            device_id_type=MESH,
        )

    rims = [(qraw, rim_q), (kraw, rim_k), (vraw, rim_v)]

    @pl.when(me < n - 1)
    def _():
        for i, (raw, rim) in enumerate(rims):
            rim_copy(raw, rim, i, later).start()

    @pl.loop(me + 1, n)
    def _(dest):
        kv_copy(kbuf, 0, me, dest).start()
        kv_copy(vbuf, 1, me, dest).start()

    row, col = iotas(rows)
    ones_low = jnp.where(row >= col, 1.0, 0.0)
    cum_s[...] = jnp.dot(ones_low, decay[...], precision=HIGHEST, preferred_element_type=F32)
    ones_up = jnp.where(row <= col, 1.0, 0.0)
    cumt_s[...] = lax.dot_general(
        decay[...], ones_up, (((0,), (0,)), ((), ())), precision=HIGHEST,
        preferred_element_type=F32,
    )

    @pl.when(me == 0)
    def _():
        for _, rim in rims:
            rim[...] = jnp.zeros_like(rim)
        in_buf[...] = jnp.zeros_like(in_buf)

    @pl.when(me > 0)
    def _():
        for i, (raw, rim) in enumerate(rims):
            rim_copy(raw, rim, i, behind).wait_recv()

    def conv_silu(slot, raw, rim, taps, cols):
        pad[slot, 0:RIM] = rim[:, cols].astype(F32)
        pad[slot, RIM : RIM + rows] = raw[:, cols].astype(F32)
        weights = taps[:, cols]
        total = None
        for j in range(CONV):
            first = RIM - (CONV - 1) + j
            term = weights[j : j + 1] * pad[slot, first : first + rows]
            total = term if total is None else total + term
        return total * sigmoid(total)

    def head_pair(kh_i, carry):
        cols = pl.ds(pl.multiple_of(kh_i * D_K, D_K), D_K)
        query = unit_rows(conv_silu(0, qraw, rim_q, cq, cols)) * D_K ** (-0.5)
        key = unit_rows(conv_silu(1, kraw, rim_k, ck, cols))
        key_t = key.T
        gram = mm(key, key_t)
        scores = mm(query, key_t)
        lane = lax.broadcasted_iota(jnp.int32, (rows, value_heads), 1)
        for r in range(REPEATS):
            h = kh_i * REPEATS + r
            vcols = pl.ds(pl.multiple_of(h * D_V, D_V), D_V)
            value = conv_silu(2 + r, vraw, rim_v, cv, vcols)
            cum = jnp.sum(jnp.where(lane == h, cum_s[...], 0.0), -1, keepdims=True)
            beta = jnp.sum(jnp.where(lane == h, beta_in[...], 0.0), -1, keepdims=True)
            out_local, state_query, offset, transfer = delta_local(
                gram, scores, key, key_t, query, value, cum, cumt_s[pl.ds(h, 1), :], beta
            )
            out_local_s[:, vcols] = out_local
            state_query_s[:, vcols] = state_query.astype(BF16)
            offset_s[h] = offset
            transfer_s[h] = transfer.astype(BF16)
            send_buf[h] = offset.astype(BF16)

        @pl.when(me == 0)
        def _():
            for r in range(REPEATS):
                state_copy(kh_i * REPEATS + r, later).start()

        return carry

    lax.fori_loop(0, key_heads, head_pair, 0)

    for load in loads[15:]:
        load.wait()

    for i in range(q_heads):
        cols = slice(i * HEAD_DIM, (i + 1) * HEAD_DIM)
        qrot[i] = rope_norm(qh[:, cols].astype(F32), qgain[...], cosine[...], sine[...])

    def relay():
        @pl.loop(0, value_heads)
        def _(h):
            state_copy(h, behind).wait_recv()

            @pl.when(me < n - 1)
            def _():
                send_buf[h] = (mm(transfer_s[h], in_buf[h]) + offset_s[h]).astype(BF16)
                state_copy(h, later).start()

    scale = HEAD_DIM ** (-0.5)

    def attend(i, block, diagonal):
        scores = mmt(qrot[i], kbuf[block]) * scale
        if diagonal:
            arow, acol = iotas(rows)
            scores = jnp.where(acol <= arow, scores, -1e30)
        top = jnp.max(scores, -1, keepdims=True)
        if diagonal:
            new = top
        else:
            old = m_s[i]
            new = jnp.maximum(old, top)
        expos = jnp.exp(scores - new)
        total = jnp.sum(expos, -1, keepdims=True)
        mixed = mm(expos, vbuf[block])
        if not diagonal:
            factor = jnp.exp(old - new)
            total = total + l_s[i] * factor
            mixed = mixed + acc_s[i] * factor
        m_s[i] = new
        l_s[i] = total
        acc_s[i] = mixed

    for i in range(q_heads):
        attend(i, me, True)

    @pl.when(me == 1)
    def _():
        relay()

    @pl.loop(0, me)
    def _(block):
        kv_copy(kbuf, 0, block, behind).wait_recv()
        kv_copy(vbuf, 1, block, behind).wait_recv()
        for i in range(q_heads):
            attend(i, block, False)

    for i in range(q_heads):
        cols = slice(i * HEAD_DIM, (i + 1) * HEAD_DIM)
        gate = sigmoid(gh[:, cols].astype(F32))
        at_v[:, cols] = (acc_s[i] / l_s[i] * gate).astype(BF16)
    at_copy = pltpu.make_async_copy(at_v, at_out, out_sem.at[0])
    at_copy.start()

    @pl.when(me > 1)
    def _():
        relay()

    gain = ngain[...]

    @pl.loop(0, value_heads)
    def _(h):
        vcols = pl.ds(pl.multiple_of(h * D_V, D_V), D_V)
        out = out_local_s[:, vcols] + mm(state_query_s[:, vcols], in_buf[h])
        normed = out * lax.rsqrt(jnp.mean(out * out, -1, keepdims=True) + 1e-06) * gain
        gate = ogate[:, vcols].astype(F32)
        dn_v[:, vcols] = (normed * (gate * sigmoid(gate))).astype(BF16)

    dn_copy = pltpu.make_async_copy(dn_v, dn_out, out_sem.at[1])
    dn_copy.start()

    @pl.when(me < n - 1)
    def _():
        for i, (raw, rim) in enumerate(rims):
            rim_copy(raw, rim, i, later).wait_send()

        @pl.loop(0, value_heads)
        def _(h):
            state_copy(h, later).wait_send()

    @pl.loop(me + 1, n)
    def _(dest):
        kv_copy(kbuf, 0, me, dest).wait_send()
        kv_copy(vbuf, 1, me, dest).wait_send()

    at_copy.wait()
    dn_copy.wait()


def rope_tables(count):
    half = HEAD_DIM // 8
    frequency = (ROPE_THETA ** (-np.arange(half, dtype=np.float64) / half)).astype(np.float32)
    angles = np.arange(count, dtype=np.float32)[:, None] * frequency[None, :]
    cosine = np.cos(angles.astype(np.float64)).astype(np.float32)
    sine = np.sin(angles.astype(np.float64)).astype(np.float32)
    one = np.ones((count, 128 - 2 * half), np.float32)
    return (
        np.concatenate([cosine, cosine, one], 1),
        np.concatenate([-sine, sine, 0 * one], 1),
    )


def body(
    query_raw, key_raw, value_raw, out_gate, conv_query, conv_key, conv_value, decay_log,
    write_beta, norm_gain, query_heads, gate_heads, key_heads, value_heads, query_gain, key_gain,
):
    n = lax.axis_size("ctx")
    rows = query_raw.shape[0]
    value_count = value_raw.shape[1] // D_V
    q_count = query_heads.shape[1] // HEAD_DIM
    cosine, sine = rope_tables(n * rows)
    ins = (
        query_raw, key_raw, value_raw, out_gate, conv_query, conv_key, conv_value, decay_log,
        write_beta, norm_gain[None], query_heads, gate_heads, key_heads, value_heads,
        query_gain[None], key_gain[None], jnp.asarray(cosine), jnp.asarray(sine),
    )
    like = lambda array: pltpu.VMEM(array.shape, array.dtype)
    scratch = [like(a) for a in ins[:12]]
    scratch += [pltpu.VMEM((rows, HEAD_DIM), BF16), like(ins[14]), like(ins[15])]
    scratch += [pltpu.VMEM((rows, 128), F32)] * 2
    scratch += [pltpu.VMEM((RIM, a.shape[1]), BF16) for a in ins[:3]]
    scratch += [
        pltpu.VMEM((2 + REPEATS, RIM + rows, 128), F32),
        pltpu.VMEM((rows, value_count), F32),
        pltpu.VMEM((value_count, rows), F32),
        pltpu.VMEM((rows, value_count * D_V), F32),
        pltpu.VMEM((rows, value_count * D_K), BF16),
        pltpu.VMEM((value_count, D_K, D_V), F32),
        pltpu.VMEM((value_count, D_K, D_K), BF16),
        pltpu.VMEM((n, rows, HEAD_DIM), BF16),
        pltpu.VMEM((n, rows, HEAD_DIM), BF16),
        pltpu.VMEM((q_count, rows, HEAD_DIM), BF16),
        pltpu.VMEM((q_count, rows, 1), F32),
        pltpu.VMEM((q_count, rows, 1), F32),
        pltpu.VMEM((q_count, rows, HEAD_DIM), F32),
        pltpu.VMEM((value_count, D_K, D_V), BF16),
        pltpu.VMEM((value_count, D_K, D_V), BF16),
        like(out_gate),
        like(gate_heads),
        pltpu.SemaphoreType.DMA((18,)),
        pltpu.SemaphoreType.DMA((3,)),
        pltpu.SemaphoreType.DMA((3,)),
        pltpu.SemaphoreType.DMA((2, n)),
        pltpu.SemaphoreType.DMA((2, n)),
        pltpu.SemaphoreType.DMA((value_count,)),
        pltpu.SemaphoreType.DMA((value_count,)),
        pltpu.SemaphoreType.DMA((2,)),
    ]
    return pl.pallas_call(
        functools.partial(kernel, n),
        out_shape=(
            jax.ShapeDtypeStruct(out_gate.shape, BF16),
            jax.ShapeDtypeStruct(gate_heads.shape, BF16),
        ),
        in_specs=[pl.BlockSpec(memory_space=pl.ANY)] * 18,
        out_specs=(pl.BlockSpec(memory_space=pl.ANY),) * 2,
        scratch_shapes=scratch,
        compiler_params=pltpu.CompilerParams(
            collective_id=0, has_side_effects=True, vmem_limit_bytes=48 * 2**20
        ),
        name="token_mixing",
    )(*ins)


def solution(mesh):
    tokens = P(("grp", "ctx"), "head")
    taps = P(None, "head")
    shared = P(("grp", "ctx"), None)
    placed = (
        tokens, tokens, tokens, tokens, taps, taps, taps, tokens, tokens, P(),
        tokens, tokens, shared, shared, P(), P(),
    )
    return jax.shard_map(
        body, mesh=mesh, in_specs=placed, out_specs=(tokens, tokens), check_vma=False
    )
```

```python
import functools

import jax
import jax.numpy as jnp
import numpy as np
from jax import lax
from jax.experimental import pallas as pl
from jax.experimental.pallas import tpu as pltpu
from jax.sharding import PartitionSpec as P

D_K = 128
D_V = 128
K_HEADS = 16
VALUE_HEAD_COUNT = 32
CONV = 4
Q_HEADS = 16
KV_HEADS = 2
HEAD_DIM = 256
ROPE_THETA = 10000000.0
REPEATS = VALUE_HEAD_COUNT // K_HEADS
RIM = 16

HIGHEST = lax.Precision.HIGHEST
MESH = pl.DeviceIdType.MESH
F32 = jnp.float32
BF16 = jnp.bfloat16


def mm(left, right):
    return jnp.dot(left.astype(BF16), right.astype(BF16), preferred_element_type=F32)


def mmt(left, right):
    return lax.dot_general(
        left.astype(BF16),
        right.astype(BF16),
        (((1,), (1,)), ((), ())),
        preferred_element_type=F32,
    )


def sigmoid(x):
    return 1.0 / (1.0 + jnp.exp(-x))


def unit_rows(x):
    return x * lax.rsqrt(jnp.sum(x * x, -1, keepdims=True) + 1e-06)


def iotas(rows):
    row = lax.broadcasted_iota(jnp.int32, (rows, rows), 0)
    col = lax.broadcasted_iota(jnp.int32, (rows, rows), 1)
    return row, col


def delta_local(heads, masks):
    lower, strict, eye, same16, same64 = masks
    identity = jnp.where(eye, 1.0, 0.0)
    withins = [
        jnp.where(lower, jnp.exp(jnp.where(lower, h["cum"] - h["cum_row"], 0.0)), 0.0)
        for h in heads
    ]
    couplings = [
        jnp.where(strict, h["beta"] * h["gram"] * within, 0.0)
        for h, within in zip(heads, withins)
    ]
    inners = [(h["scores"] * within).astype(BF16) for h, within in zip(heads, withins)]
    rest16 = [jnp.where(same64 & ~same16, c, 0.0).astype(BF16) for c in couplings]
    rest64 = [jnp.where(same64, 0.0, c).astype(BF16) for c in couplings]

    powers = [jnp.where(same16, -c, 0.0) for c in couplings]
    inverses = [(identity + p).astype(BF16) for p in powers]
    powers = [p.astype(BF16) for p in powers]
    for _ in range(3):
        squares = [mm(p, p) for p in powers]
        factors = [(identity + p).astype(BF16) for p in squares]
        powers = [p.astype(BF16) for p in squares]
        inverses = [mm(i, f).astype(BF16) for i, f in zip(inverses, factors)]

    steps = [-mm(i, r) for i, r in zip(inverses, rest16)]
    seconds = [mm(p, p) for p in steps]
    grows = [
        mm(identity + p, identity + p2).astype(BF16) for p, p2 in zip(steps, seconds)
    ]
    inverses = [mm(g, i).astype(BF16) for g, i in zip(grows, inverses)]

    steps = [(-mm(i, r)).astype(BF16) for i, r in zip(inverses, rest64)]
    seconds = [mm(p, p).astype(BF16) for p in steps]
    decays = [jnp.exp(h["cum"]) for h in heads]
    rights = [
        jnp.concatenate([h["beta"] * h["value"], (h["beta"] * d) * h["key"]], -1)
        for h, d in zip(heads, decays)
    ]
    solved = [mm(i, r) for i, r in zip(inverses, rights)]
    solved = [x + mm(p, x) for x, p in zip(solved, seconds)]
    solved = [(x + mm(p, x)).astype(BF16) for x, p in zip(solved, steps)]

    lasts = [h["cum"][h["cum"].shape[0] - 1 :, :] for h in heads]
    ended = [
        mm(h["key_t"] * jnp.exp(last - h["cum_row"]), x)
        for h, last, x in zip(heads, lasts, solved)
    ]
    boths = [mm(inner, x) for inner, x in zip(inners, solved)]
    krow, kcol = iotas(D_K)
    results = []
    for h, d, last, end, both in zip(heads, decays, lasts, ended, boths):
        transfer = jnp.where(krow == kcol, jnp.exp(last), 0.0) - end[:, D_V:]
        results.append(
            (both[:, :D_V], h["query"] * d - both[:, D_V:], end[:, :D_V], transfer)
        )
    return results


def rope_norm(x, gain, cosine, sine):
    normed = x * lax.rsqrt(jnp.mean(x * x, -1, keepdims=True) + 1e-06) * gain
    half = HEAD_DIM // 8
    front = normed[:, :128]
    lane = lax.broadcasted_iota(jnp.int32, front.shape, 1)
    partner = jnp.where(lane < half, pltpu.roll(front, 128 - half, 1), pltpu.roll(front, half, 1))
    front = front * cosine + partner * sine
    return jnp.concatenate([front, normed[:, 128:]], -1).astype(BF16)


def kernel(n, *refs):
    ins = refs[:18]
    (
        qraw_h, kraw_h, vraw_h, ogate_h, cq_h, ck_h, cv_h, decay_h, beta_h, ngain_h,
        qh_h, gh_h, kh_h, vh_h, qgain_h, kgain_h, cos_h, sin_h,
    ) = ins
    dn_out, at_out = refs[18:20]
    (
        qraw, kraw, vraw, ogate, cq, ck, cv, decay, beta_in, ngain,
        qh, gh, kh, qgain, kgain, cosine, sine,
        rim_q, rim_k, rim_v, pad, cum_s, beta_s, cumt_s,
        out_local_s, state_query_s, offset_s, transfer_s,
        kv, qrot, m_s, l_s, acc_s, in_buf, send_buf, dn_v, at_v,
        load_sem, rim_send, rim_recv, kv_send, kv_recv, pass_send, pass_recv, st_send, st_recv, out_sem,
    ) = refs[20:]
    rows = qraw.shape[0]
    me = lax.axis_index("ctx")
    head = lax.axis_index("head")
    later = jnp.minimum(me + 1, n - 1)
    behind = jnp.maximum(me - 1, 0)
    core = lax.rem(head, 2)
    peer = head + 1 - 2 * core
    key_heads = qraw.shape[1] // D_K
    value_heads = vraw.shape[1] // D_V
    q_heads = qh.shape[1] // HEAD_DIM
    kv_index = head * q_heads // (Q_HEADS // KV_HEADS)
    kv_cols = pl.ds(pl.multiple_of(kv_index * HEAD_DIM, HEAD_DIM), HEAD_DIM)
    own_rows = pl.ds(pl.multiple_of(me * rows, rows), rows)

    barrier = pltpu.get_barrier_semaphore()

    @pl.loop(1, n)
    def _(d):
        pl.semaphore_signal(
            barrier, inc=1, device_id={"ctx": lax.rem(me + d, n)}, device_id_type=MESH
        )

    pl.semaphore_signal(barrier, inc=1, device_id={"head": peer}, device_id_type=MESH)

    pairs = [
        (kh_h.at[:, kv_cols], kh),
        (cos_h.at[own_rows], cosine),
        (sin_h.at[own_rows], sine),
        (kgain_h, kgain),
        (vh_h.at[:, kv_cols], kv.at[1, me]),
        (qraw_h, qraw),
        (kraw_h, kraw),
        (vraw_h, vraw),
        (decay_h, decay),
        (beta_h, beta_in),
        (cq_h, cq),
        (ck_h, ck),
        (cv_h, cv),
        (ngain_h, ngain),
        (qgain_h, qgain),
        (qh_h, qh),
        (gh_h, gh),
        (ogate_h, ogate),
    ]
    loads = [
        pltpu.make_async_copy(source, target, load_sem.at[i])
        for i, (source, target) in enumerate(pairs)
    ]
    for load in loads:
        load.start()

    for load in loads[:5]:
        load.wait()
    kv[0, me] = rope_norm(kh[...].astype(F32), kgain[...], cosine[...], sine[...])
    for load in loads[5:15]:
        load.wait()
    pl.semaphore_wait(barrier, n)

    def rim_copy(raw, rim, i, dest):
        return pltpu.make_async_remote_copy(
            src_ref=raw.at[pl.ds(rows - RIM, RIM)],
            dst_ref=rim,
            send_sem=rim_send.at[i],
            recv_sem=rim_recv.at[i],
            device_id={"ctx": dest},
            device_id_type=MESH,
        )

    def kv_copy(block, dest):
        return pltpu.make_async_remote_copy(
            src_ref=kv.at[core, block],
            dst_ref=kv.at[core, block],
            send_sem=kv_send.at[dest],
            recv_sem=kv_recv.at[block],
            device_id={"ctx": dest},
            device_id_type=MESH,
        )

    def pass_copy(which, block):
        return pltpu.make_async_remote_copy(
            src_ref=kv.at[which, block],
            dst_ref=kv.at[which, block],
            send_sem=pass_send.at[block],
            recv_sem=pass_recv.at[block],
            device_id={"head": peer},
            device_id_type=MESH,
        )

    def state_copy(h, dest):
        return pltpu.make_async_remote_copy(
            src_ref=send_buf.at[h],
            dst_ref=in_buf.at[h],
            send_sem=st_send.at[h],
            recv_sem=st_recv.at[h],
            device_id={"ctx": dest},
            device_id_type=MESH,
        )

    rims = [(qraw, rim_q), (kraw, rim_k), (vraw, rim_v)]

    @pl.when(me < n - 1)
    def _():
        for i, (raw, rim) in enumerate(rims):
            rim_copy(raw, rim, i, later).start()

    @pl.loop(me + 1, n)
    def _(dest):
        kv_copy(me, dest).start()

    row, col = iotas(rows)
    ones_low = jnp.where(row >= col, 1.0, 0.0)
    ones_up = jnp.where(row <= col, 1.0, 0.0)
    cumt_s[...] = jnp.dot(decay[...], ones_up, precision=HIGHEST, preferred_element_type=F32)
    cum_s[...] = lax.dot_general(
        ones_low, decay[...], (((1,), (1,)), ((), ())), precision=HIGHEST,
        preferred_element_type=F32,
    )
    beta_s[...] = beta_in[...].T

    @pl.when(me == 0)
    def _():
        for _, rim in rims:
            rim[...] = jnp.zeros_like(rim)
        in_buf[...] = jnp.zeros_like(in_buf)

    @pl.when(me > 0)
    def _():
        for i, (raw, rim) in enumerate(rims):
            rim_copy(raw, rim, i, behind).wait_recv()

    def conv_silu(slot, raw, rim, taps, cols):
        pad[slot, 0:RIM] = rim[:, cols].astype(F32)
        pad[slot, RIM : RIM + rows] = raw[:, cols].astype(F32)
        weights = taps[:, cols]
        total = None
        for j in range(CONV):
            first = RIM - (CONV - 1) + j
            term = weights[j : j + 1] * pad[slot, first : first + rows]
            total = term if total is None else total + term
        return total * sigmoid(total)

    group = 2 if key_heads % 2 == 0 else 1

    def head_group(g, carry):
        lane = lax.broadcasted_iota(jnp.int32, (rows, value_heads), 1)
        mrow, mcol = iotas(rows)
        masks = (
            mrow >= mcol, mrow > mcol, mrow == mcol,
            (mrow // 16) == (mcol // 16), (mrow // 64) == (mcol // 64),
        )
        heads = []
        for i in range(group):
            kh_i = g * group + i
            cols = pl.ds(pl.multiple_of(kh_i * D_K, D_K), D_K)
            slot = i * (2 + REPEATS)
            query = unit_rows(conv_silu(slot, qraw, rim_q, cq, cols)) * D_K ** (-0.5)
            key = unit_rows(conv_silu(slot + 1, kraw, rim_k, ck, cols))
            key_t = key.T
            gram = mm(key, key_t)
            scores = mm(query, key_t)
            for r in range(REPEATS):
                h = kh_i * REPEATS + r
                vcols = pl.ds(pl.multiple_of(h * D_V, D_V), D_V)
                heads.append(dict(
                    h=h, vcols=vcols, query=query, key=key, key_t=key_t, gram=gram,
                    scores=scores,
                    value=conv_silu(slot + 2 + r, vraw, rim_v, cv, vcols),
                    cum=jnp.sum(jnp.where(lane == h, cum_s[...], 0.0), -1, keepdims=True),
                    beta=jnp.sum(jnp.where(lane == h, beta_s[...], 0.0), -1, keepdims=True),
                    cum_row=cumt_s[pl.ds(h, 1), :],
                ))
        results = delta_local(heads, masks)
        for item, (out_local, state_query, offset, transfer) in zip(heads, results):
            h, vcols = item["h"], item["vcols"]
            out_local_s[:, vcols] = out_local
            state_query_s[:, vcols] = state_query.astype(BF16)
            offset_s[h] = offset
            transfer_s[h] = transfer.astype(BF16)
            send_buf[h] = offset.astype(BF16)

        @pl.when(me == 0)
        def _():
            for i in range(group * REPEATS):
                state_copy(g * group * REPEATS + i, later).start()

        return carry

    lax.fori_loop(0, key_heads // group, head_group, 0)

    @pl.loop(0, me)
    def _(block):
        kv_copy(block, behind).wait_recv()
        pass_copy(core, block).start()

    for load in loads[15:]:
        load.wait()

    for i in range(q_heads):
        cols = slice(i * HEAD_DIM, (i + 1) * HEAD_DIM)
        qrot[i] = rope_norm(qh[:, cols].astype(F32), qgain[...], cosine[...], sine[...])

    def relay():
        @pl.loop(0, value_heads)
        def _(h):
            state_copy(h, behind).wait_recv()

            @pl.when(me < n - 1)
            def _():
                send_buf[h] = (mm(transfer_s[h], in_buf[h]) + offset_s[h]).astype(BF16)
                state_copy(h, later).start()

    scale = HEAD_DIM ** (-0.5)

    def attend(i, block, diagonal):
        scores = mmt(qrot[i], kv[0, block]) * scale
        if diagonal:
            arow, acol = iotas(rows)
            scores = jnp.where(acol <= arow, scores, -1e30)
        top = jnp.max(scores, -1, keepdims=True)
        if diagonal:
            new = top
        else:
            old = m_s[i]
            new = jnp.maximum(old, top)
        expos = jnp.exp(scores - new)
        total = jnp.sum(expos, -1, keepdims=True)
        mixed = mm(expos, kv[1, block])
        if not diagonal:
            factor = jnp.exp(old - new)
            total = total + l_s[i] * factor
            mixed = mixed + acc_s[i] * factor
        m_s[i] = new
        l_s[i] = total
        acc_s[i] = mixed

    for i in range(q_heads):
        attend(i, me, True)

    @pl.when(me == 1)
    def _():
        relay()

    @pl.loop(0, me)
    def _(block):
        pass_copy(1 - core, block).wait_recv()
        for i in range(q_heads):
            attend(i, block, False)

    for i in range(q_heads):
        cols = slice(i * HEAD_DIM, (i + 1) * HEAD_DIM)
        gate = sigmoid(gh[:, cols].astype(F32))
        at_v[:, cols] = (acc_s[i] / l_s[i] * gate).astype(BF16)
    at_copy = pltpu.make_async_copy(at_v, at_out, out_sem.at[0])
    at_copy.start()

    @pl.when(me > 1)
    def _():
        relay()

    gain = ngain[...]

    @pl.loop(0, value_heads)
    def _(h):
        vcols = pl.ds(pl.multiple_of(h * D_V, D_V), D_V)
        out = out_local_s[:, vcols] + mm(state_query_s[:, vcols], in_buf[h])
        normed = out * lax.rsqrt(jnp.mean(out * out, -1, keepdims=True) + 1e-06) * gain
        gate = ogate[:, vcols].astype(F32)
        dn_v[:, vcols] = (normed * (gate * sigmoid(gate))).astype(BF16)

    dn_copy = pltpu.make_async_copy(dn_v, dn_out, out_sem.at[1])
    dn_copy.start()

    @pl.when(me < n - 1)
    def _():
        for i, (raw, rim) in enumerate(rims):
            rim_copy(raw, rim, i, later).wait_send()

        @pl.loop(0, value_heads)
        def _(h):
            state_copy(h, later).wait_send()

    @pl.loop(me + 1, n)
    def _(dest):
        kv_copy(me, dest).wait_send()

    @pl.loop(0, me)
    def _(block):
        pass_copy(core, block).wait_send()

    at_copy.wait()
    dn_copy.wait()


def rope_tables(count):
    half = HEAD_DIM // 8
    frequency = (ROPE_THETA ** (-np.arange(half, dtype=np.float64) / half)).astype(np.float32)
    angles = np.arange(count, dtype=np.float32)[:, None] * frequency[None, :]
    cosine = np.cos(angles.astype(np.float64)).astype(np.float32)
    sine = np.sin(angles.astype(np.float64)).astype(np.float32)
    one = np.ones((count, 128 - 2 * half), np.float32)
    return (
        np.concatenate([cosine, cosine, one], 1),
        np.concatenate([-sine, sine, 0 * one], 1),
    )


def body(
    query_raw, key_raw, value_raw, out_gate, conv_query, conv_key, conv_value, decay_log,
    write_beta, norm_gain, query_heads, gate_heads, key_heads, value_heads, query_gain, key_gain,
):
    n = lax.axis_size("ctx")
    rows = query_raw.shape[0]
    value_count = value_raw.shape[1] // D_V
    q_count = query_heads.shape[1] // HEAD_DIM
    cosine, sine = rope_tables(n * rows)
    ins = (
        query_raw, key_raw, value_raw, out_gate, conv_query, conv_key, conv_value, decay_log.T,
        write_beta.T, norm_gain[None], query_heads, gate_heads, key_heads, value_heads,
        query_gain[None], key_gain[None], jnp.asarray(cosine), jnp.asarray(sine),
    )
    like = lambda array: pltpu.VMEM(array.shape, array.dtype)
    scratch = [like(a) for a in ins[:12]]
    scratch += [pltpu.VMEM((rows, HEAD_DIM), BF16), like(ins[14]), like(ins[15])]
    scratch += [pltpu.VMEM((rows, 128), F32)] * 2
    scratch += [pltpu.VMEM((RIM, a.shape[1]), BF16) for a in ins[:3]]
    scratch += [
        pltpu.VMEM((2 * (2 + REPEATS), RIM + rows, 128), F32),
        pltpu.VMEM((rows, value_count), F32),
        pltpu.VMEM((rows, value_count), F32),
        pltpu.VMEM((value_count, rows), F32),
        pltpu.VMEM((rows, value_count * D_V), F32),
        pltpu.VMEM((rows, value_count * D_K), BF16),
        pltpu.VMEM((value_count, D_K, D_V), F32),
        pltpu.VMEM((value_count, D_K, D_K), BF16),
        pltpu.VMEM((2, n, rows, HEAD_DIM), BF16),
        pltpu.VMEM((q_count, rows, HEAD_DIM), BF16),
        pltpu.VMEM((q_count, rows, 1), F32),
        pltpu.VMEM((q_count, rows, 1), F32),
        pltpu.VMEM((q_count, rows, HEAD_DIM), F32),
        pltpu.VMEM((value_count, D_K, D_V), BF16),
        pltpu.VMEM((value_count, D_K, D_V), BF16),
        like(out_gate),
        like(gate_heads),
        pltpu.SemaphoreType.DMA((18,)),
        pltpu.SemaphoreType.DMA((3,)),
        pltpu.SemaphoreType.DMA((3,)),
        pltpu.SemaphoreType.DMA((n,)),
        pltpu.SemaphoreType.DMA((n,)),
        pltpu.SemaphoreType.DMA((n,)),
        pltpu.SemaphoreType.DMA((n,)),
        pltpu.SemaphoreType.DMA((value_count,)),
        pltpu.SemaphoreType.DMA((value_count,)),
        pltpu.SemaphoreType.DMA((2,)),
    ]
    return pl.pallas_call(
        functools.partial(kernel, n),
        out_shape=(
            jax.ShapeDtypeStruct(out_gate.shape, BF16),
            jax.ShapeDtypeStruct(gate_heads.shape, BF16),
        ),
        in_specs=[pl.BlockSpec(memory_space=pl.ANY)] * 18,
        out_specs=(pl.BlockSpec(memory_space=pl.ANY),) * 2,
        scratch_shapes=scratch,
        compiler_params=pltpu.CompilerParams(
            collective_id=0, has_side_effects=True, vmem_limit_bytes=60 * 2**20
        ),
        name="token_mixing",
    )(*ins)


def solution(mesh):
    tokens = P(("grp", "ctx"), "head")
    taps = P(None, "head")
    shared = P(("grp", "ctx"), None)
    placed = (
        tokens, tokens, tokens, tokens, taps, taps, taps, tokens, tokens, P(),
        tokens, tokens, shared, shared, P(), P(),
    )
    return jax.shard_map(
        body, mesh=mesh, in_specs=placed, out_specs=(tokens, tokens), check_vma=False
    )
```

```python
import functools

import jax
import jax.numpy as jnp
import numpy as np
from jax import lax
from jax.experimental import pallas as pl
from jax.experimental.pallas import tpu as pltpu
from jax.sharding import PartitionSpec as P

D_K = 128
D_V = 128
K_HEADS = 16
VALUE_HEAD_COUNT = 32
CONV = 4
Q_HEADS = 16
KV_HEADS = 2
HEAD_DIM = 256
ROPE_THETA = 10000000.0
REPEATS = VALUE_HEAD_COUNT // K_HEADS
RIM = 16

HIGHEST = lax.Precision.HIGHEST
MESH = pl.DeviceIdType.MESH
F32 = jnp.float32
BF16 = jnp.bfloat16


def mm(left, right):
    return jnp.dot(left.astype(BF16), right.astype(BF16), preferred_element_type=F32)


def mmt(left, right):
    return lax.dot_general(
        left.astype(BF16),
        right.astype(BF16),
        (((1,), (1,)), ((), ())),
        preferred_element_type=F32,
    )


def sigmoid(x):
    return 1.0 / (1.0 + jnp.exp(-x))


def unit_rows(x):
    return x * lax.rsqrt(jnp.sum(x * x, -1, keepdims=True) + 1e-06)


def iotas(rows):
    row = lax.broadcasted_iota(jnp.int32, (rows, rows), 0)
    col = lax.broadcasted_iota(jnp.int32, (rows, rows), 1)
    return row, col


def delta_local(heads, masks):
    lower, strict, eye, same16, same64 = masks
    identity = jnp.where(eye, 1.0, 0.0)
    withins = [
        jnp.where(lower, jnp.exp(jnp.where(lower, h["cum"] - h["cum_row"], 0.0)), 0.0)
        for h in heads
    ]
    couplings = [
        jnp.where(strict, h["beta"] * h["gram"] * within, 0.0)
        for h, within in zip(heads, withins)
    ]
    inners = [(h["scores"] * within).astype(BF16) for h, within in zip(heads, withins)]
    rest16 = [jnp.where(same64 & ~same16, c, 0.0).astype(BF16) for c in couplings]
    rest64 = [jnp.where(same64, 0.0, c).astype(BF16) for c in couplings]

    powers = [jnp.where(same16, -c, 0.0) for c in couplings]
    inverses = [(identity + p).astype(BF16) for p in powers]
    powers = [p.astype(BF16) for p in powers]
    for _ in range(3):
        squares = [mm(p, p) for p in powers]
        factors = [(identity + p).astype(BF16) for p in squares]
        powers = [p.astype(BF16) for p in squares]
        inverses = [mm(i, f).astype(BF16) for i, f in zip(inverses, factors)]

    steps = [-mm(i, r) for i, r in zip(inverses, rest16)]
    seconds = [mm(p, p) for p in steps]
    grows = [
        mm(identity + p, identity + p2).astype(BF16) for p, p2 in zip(steps, seconds)
    ]
    inverses = [mm(g, i).astype(BF16) for g, i in zip(grows, inverses)]

    steps = [(-mm(i, r)).astype(BF16) for i, r in zip(inverses, rest64)]
    seconds = [mm(p, p).astype(BF16) for p in steps]
    decays = [jnp.exp(h["cum"]) for h in heads]
    rights = [
        jnp.concatenate([h["beta"] * h["value"], (h["beta"] * d) * h["key"]], -1)
        for h, d in zip(heads, decays)
    ]
    solved = [mm(i, r) for i, r in zip(inverses, rights)]
    solved = [x + mm(p, x) for x, p in zip(solved, seconds)]
    solved = [(x + mm(p, x)).astype(BF16) for x, p in zip(solved, steps)]

    lasts = [h["cum"][h["cum"].shape[0] - 1 :, :] for h in heads]
    ended = [
        mm(h["key_t"] * jnp.exp(last - h["cum_row"]), x)
        for h, last, x in zip(heads, lasts, solved)
    ]
    boths = [mm(inner, x) for inner, x in zip(inners, solved)]
    krow, kcol = iotas(D_K)
    results = []
    for h, d, last, end, both in zip(heads, decays, lasts, ended, boths):
        transfer = jnp.where(krow == kcol, jnp.exp(last), 0.0) - end[:, D_V:]
        results.append(
            (both[:, :D_V], h["query"] * d - both[:, D_V:], end[:, :D_V], transfer)
        )
    return results


def rope_norm(x, gain, cosine, sine):
    normed = x * lax.rsqrt(jnp.mean(x * x, -1, keepdims=True) + 1e-06) * gain
    half = HEAD_DIM // 8
    front = normed[:, :128]
    lane = lax.broadcasted_iota(jnp.int32, front.shape, 1)
    partner = jnp.where(lane < half, pltpu.roll(front, 128 - half, 1), pltpu.roll(front, half, 1))
    front = front * cosine + partner * sine
    return jnp.concatenate([front, normed[:, 128:]], -1).astype(BF16)


def kernel(n, *refs):
    ins = refs[:18]
    (
        qraw_h, kraw_h, vraw_h, ogate_h, cq_h, ck_h, cv_h, decay_h, beta_h, ngain_h,
        qh_h, gh_h, kh_h, vh_h, qgain_h, kgain_h, cos_h, sin_h,
    ) = ins
    dn_out, at_out = refs[18:20]
    (
        qraw, kraw, vraw, ogate, cq, ck, cv, decay, beta_in, ngain,
        qh, gh, kh, qgain, kgain, cosine, sine,
        rim_q, rim_k, rim_v, pad, cum_s, beta_s, cumt_s,
        out_local_s, state_query_s, offset_s, transfer_s,
        kv, qrot, m_s, l_s, acc_s, in_buf, send_buf, dn_v, at_v,
        load_sem, rim_send, rim_recv, kv_send, kv_recv, pass_send, pass_recv, st_send, st_recv, out_sem,
    ) = refs[20:]
    rows = qraw.shape[0]
    me = lax.axis_index("ctx")
    head = lax.axis_index("head")
    later = jnp.minimum(me + 1, n - 1)
    behind = jnp.maximum(me - 1, 0)
    core = lax.rem(head, 2)
    peer = head + 1 - 2 * core
    key_heads = qraw.shape[1] // D_K
    value_heads = vraw.shape[1] // D_V
    q_heads = qh.shape[1] // HEAD_DIM
    kv_index = head * q_heads // (Q_HEADS // KV_HEADS)
    kv_cols = pl.ds(pl.multiple_of(kv_index * HEAD_DIM, HEAD_DIM), HEAD_DIM)
    own_rows = pl.ds(pl.multiple_of(me * rows, rows), rows)

    barrier = pltpu.get_barrier_semaphore()

    @pl.when(me > 0)
    def _():
        pl.semaphore_signal(barrier, inc=1, device_id={"ctx": behind}, device_id_type=MESH)

    pl.semaphore_signal(barrier, inc=1, device_id={"head": peer}, device_id_type=MESH)

    pairs = [
        (kh_h.at[:, kv_cols], kh),
        (cos_h.at[own_rows], cosine),
        (sin_h.at[own_rows], sine),
        (kgain_h, kgain),
        (vh_h.at[:, kv_cols], kv.at[1, me]),
        (qgain_h, qgain),
        (qh_h, qh),
        (qraw_h, qraw),
        (kraw_h, kraw),
        (vraw_h, vraw),
        (decay_h, decay),
        (beta_h, beta_in),
        (cq_h, cq),
        (ck_h, ck),
        (cv_h, cv),
        (ngain_h, ngain),
        (gh_h, gh),
        (ogate_h, ogate),
    ]
    loads = [
        pltpu.make_async_copy(source, target, load_sem.at[i])
        for i, (source, target) in enumerate(pairs)
    ]
    for load in loads:
        load.start()

    def rim_copy(raw, rim, i, dest):
        return pltpu.make_async_remote_copy(
            src_ref=raw.at[pl.ds(rows - RIM, RIM)],
            dst_ref=rim,
            send_sem=rim_send.at[i],
            recv_sem=rim_recv.at[i],
            device_id={"ctx": dest},
            device_id_type=MESH,
        )

    def kv_copy(block, dest):
        return pltpu.make_async_remote_copy(
            src_ref=kv.at[core, block],
            dst_ref=kv.at[core, block],
            send_sem=kv_send.at[block],
            recv_sem=kv_recv.at[block],
            device_id={"ctx": dest},
            device_id_type=MESH,
        )

    def pass_copy(which, block):
        return pltpu.make_async_remote_copy(
            src_ref=kv.at[which, block],
            dst_ref=kv.at[which, block],
            send_sem=pass_send.at[block],
            recv_sem=pass_recv.at[block],
            device_id={"head": peer},
            device_id_type=MESH,
        )

    def state_copy(h, dest):
        return pltpu.make_async_remote_copy(
            src_ref=send_buf.at[h],
            dst_ref=in_buf.at[h],
            send_sem=st_send.at[h],
            recv_sem=st_recv.at[h],
            device_id={"ctx": dest},
            device_id_type=MESH,
        )

    rims = [(qraw_h, rim_q), (kraw_h, rim_k), (vraw_h, rim_v)]

    pl.semaphore_wait(barrier, 1 + later - me)

    @pl.when(me < n - 1)
    def _():
        for i, (raw, rim) in enumerate(rims):
            rim_copy(raw, rim, i, later).start()

    for load in loads[:5]:
        load.wait()
    kv[0, me] = rope_norm(kh[...].astype(F32), kgain[...], cosine[...], sine[...])

    @pl.when(me < n - 1)
    def _():
        kv_copy(me, later).start()

    for load in loads[5:17]:
        load.wait()

    row, col = iotas(rows)
    ones_low = jnp.where(row >= col, 1.0, 0.0)
    ones_up = jnp.where(row <= col, 1.0, 0.0)
    cumt_s[...] = jnp.dot(decay[...], ones_up, precision=HIGHEST, preferred_element_type=F32)
    cum_s[...] = lax.dot_general(
        ones_low, decay[...], (((1,), (1,)), ((), ())), precision=HIGHEST,
        preferred_element_type=F32,
    )
    beta_s[...] = beta_in[...].T

    @pl.when(me == 0)
    def _():
        for _, rim in rims:
            rim[...] = jnp.zeros_like(rim)
        in_buf[...] = jnp.zeros_like(in_buf)

    scale = HEAD_DIM ** (-0.5)

    def attend(i, block, diagonal):
        scores = mmt(qrot[i], kv[0, block]) * scale
        if diagonal:
            arow, acol = iotas(rows)
            scores = jnp.where(acol <= arow, scores, -1e30)
        top = jnp.max(scores, -1, keepdims=True)
        if diagonal:
            new = top
        else:
            old = m_s[i]
            new = jnp.maximum(old, top)
        expos = jnp.exp(scores - new)
        total = jnp.sum(expos, -1, keepdims=True)
        mixed = mm(expos, kv[1, block])
        if not diagonal:
            factor = jnp.exp(old - new)
            total = total + l_s[i] * factor
            mixed = mixed + acc_s[i] * factor
        m_s[i] = new
        l_s[i] = total
        acc_s[i] = mixed

    def own_block():
        for i in range(q_heads):
            cols = slice(i * HEAD_DIM, (i + 1) * HEAD_DIM)
            qrot[i] = rope_norm(qh[:, cols].astype(F32), qgain[...], cosine[...], sine[...])
            attend(i, me, True)

    @pl.when(me > 0)
    def _():
        own_block()
        for i, (raw, rim) in enumerate(rims):
            rim_copy(raw, rim, i, behind).wait_recv()

    def conv_silu(slot, raw, rim, taps, cols):
        pad[slot, 0:RIM] = rim[:, cols].astype(F32)
        pad[slot, RIM : RIM + rows] = raw[:, cols].astype(F32)
        weights = taps[:, cols]
        total = None
        for j in range(CONV):
            first = RIM - (CONV - 1) + j
            term = weights[j : j + 1] * pad[slot, first : first + rows]
            total = term if total is None else total + term
        return total * sigmoid(total)

    group = 2 if key_heads % 2 == 0 else 1
    groups = key_heads // group

    def ring_step(step):
        block = me - step
        kv_copy(block, behind).wait_recv()
        pass_copy(core, block).start()

        @pl.when(me < n - 1)
        def _():
            kv_copy(block, later).start()

    def head_group(g, carry):
        lane = lax.broadcasted_iota(jnp.int32, (rows, value_heads), 1)
        mrow, mcol = iotas(rows)
        masks = (
            mrow >= mcol, mrow > mcol, mrow == mcol,
            (mrow // 16) == (mcol // 16), (mrow // 64) == (mcol // 64),
        )
        heads = []
        for i in range(group):
            kh_i = g * group + i
            cols = pl.ds(pl.multiple_of(kh_i * D_K, D_K), D_K)
            slot = i * (2 + REPEATS)
            query = unit_rows(conv_silu(slot, qraw, rim_q, cq, cols)) * D_K ** (-0.5)
            key = unit_rows(conv_silu(slot + 1, kraw, rim_k, ck, cols))
            key_t = key.T
            gram = mm(key, key_t)
            scores = mm(query, key_t)
            for r in range(REPEATS):
                h = kh_i * REPEATS + r
                vcols = pl.ds(pl.multiple_of(h * D_V, D_V), D_V)
                heads.append(dict(
                    h=h, vcols=vcols, query=query, key=key, key_t=key_t, gram=gram,
                    scores=scores,
                    value=conv_silu(slot + 2 + r, vraw, rim_v, cv, vcols),
                    cum=jnp.sum(jnp.where(lane == h, cum_s[...], 0.0), -1, keepdims=True),
                    beta=jnp.sum(jnp.where(lane == h, beta_s[...], 0.0), -1, keepdims=True),
                    cum_row=cumt_s[pl.ds(h, 1), :],
                ))
        results = delta_local(heads, masks)
        for item, (out_local, state_query, offset, transfer) in zip(heads, results):
            h, vcols = item["h"], item["vcols"]
            out_local_s[:, vcols] = out_local
            state_query_s[:, vcols] = state_query.astype(BF16)
            offset_s[h] = offset
            transfer_s[h] = transfer.astype(BF16)
            send_buf[h] = offset.astype(BF16)

        @pl.when(me == 0)
        def _():
            for i in range(group * REPEATS):
                state_copy(g * group * REPEATS + i, later).start()

        @pl.when(g + 1 <= me)
        def _():
            ring_step(g + 1)

        return carry

    lax.fori_loop(0, groups, head_group, 0)

    def relay(first, count):
        @pl.loop(first, first + count)
        def _(h):
            state_copy(h, behind).wait_recv()

            @pl.when(me < n - 1)
            def _():
                send_buf[h] = (mm(transfer_s[h], in_buf[h]) + offset_s[h]).astype(BF16)
                state_copy(h, later).start()

    half = value_heads // 2

    @pl.when(me == 0)
    def _():
        own_block()

    @pl.when(me == 1)
    def _():
        relay(0, half)

    @pl.loop(1, me + 1)
    def _(step):
        @pl.when(step > groups)
        def _():
            ring_step(step)

        pass_copy(1 - core, me - step).wait_recv()
        for i in range(q_heads):
            attend(i, me - step, False)

    @pl.when(me > 1)
    def _():
        relay(0, half)

    @pl.when(me > 0)
    def _():
        relay(half, value_heads - half)

    for load in loads[17:]:
        load.wait()

    for i in range(q_heads):
        cols = slice(i * HEAD_DIM, (i + 1) * HEAD_DIM)
        gate = sigmoid(gh[:, cols].astype(F32))
        at_v[:, cols] = (acc_s[i] / l_s[i] * gate).astype(BF16)
    at_copy = pltpu.make_async_copy(at_v, at_out, out_sem.at[0])
    at_copy.start()

    gain = ngain[...]

    @pl.loop(0, value_heads)
    def _(h):
        vcols = pl.ds(pl.multiple_of(h * D_V, D_V), D_V)
        out = out_local_s[:, vcols] + mm(state_query_s[:, vcols], in_buf[h])
        normed = out * lax.rsqrt(jnp.mean(out * out, -1, keepdims=True) + 1e-06) * gain
        gate = ogate[:, vcols].astype(F32)
        dn_v[:, vcols] = (normed * (gate * sigmoid(gate))).astype(BF16)

    dn_copy = pltpu.make_async_copy(dn_v, dn_out, out_sem.at[1])
    dn_copy.start()

    @pl.when(me < n - 1)
    def _():
        for i, (raw, rim) in enumerate(rims):
            rim_copy(raw, rim, i, later).wait_send()

        @pl.loop(0, value_heads)
        def _(h):
            state_copy(h, later).wait_send()

        @pl.loop(0, me + 1)
        def _(block):
            kv_copy(block, later).wait_send()

    @pl.loop(0, me)
    def _(block):
        pass_copy(core, block).wait_send()

    at_copy.wait()
    dn_copy.wait()


def place(first, second, first_out, second_out, sem):
    copies = [
        pltpu.make_async_copy(first, first_out, sem.at[0]),
        pltpu.make_async_copy(second, second_out, sem.at[1]),
    ]
    for copy in copies:
        copy.start()
    for copy in copies:
        copy.wait()


def rope_tables(count):
    half = HEAD_DIM // 8
    frequency = (ROPE_THETA ** (-np.arange(half, dtype=np.float64) / half)).astype(np.float32)
    angles = np.arange(count, dtype=np.float32)[:, None] * frequency[None, :]
    cosine = np.cos(angles.astype(np.float64)).astype(np.float32)
    sine = np.sin(angles.astype(np.float64)).astype(np.float32)
    one = np.ones((count, 128 - 2 * half), np.float32)
    return (
        np.concatenate([cosine, cosine, one], 1),
        np.concatenate([-sine, sine, 0 * one], 1),
    )


def body(
    query_raw, key_raw, value_raw, out_gate, conv_query, conv_key, conv_value, decay_log,
    write_beta, norm_gain, query_heads, gate_heads, key_heads, value_heads, query_gain, key_gain,
):
    n = lax.axis_size("ctx")
    rows = query_raw.shape[0]
    value_count = value_raw.shape[1] // D_V
    q_count = query_heads.shape[1] // HEAD_DIM
    cosine, sine = rope_tables(n * rows)
    ins = (
        query_raw, key_raw, value_raw, out_gate, conv_query, conv_key, conv_value, decay_log.T,
        write_beta.T, norm_gain[None], query_heads, gate_heads, key_heads, value_heads,
        query_gain[None], key_gain[None], jnp.asarray(cosine), jnp.asarray(sine),
    )
    like = lambda array: pltpu.VMEM(array.shape, array.dtype)
    scratch = [like(a) for a in ins[:12]]
    scratch += [pltpu.VMEM((rows, HEAD_DIM), BF16), like(ins[14]), like(ins[15])]
    scratch += [pltpu.VMEM((rows, 128), F32)] * 2
    scratch += [pltpu.VMEM((RIM, a.shape[1]), BF16) for a in ins[:3]]
    scratch += [
        pltpu.VMEM((2 * (2 + REPEATS), RIM + rows, 128), F32),
        pltpu.VMEM((rows, value_count), F32),
        pltpu.VMEM((rows, value_count), F32),
        pltpu.VMEM((value_count, rows), F32),
        pltpu.VMEM((rows, value_count * D_V), F32),
        pltpu.VMEM((rows, value_count * D_K), BF16),
        pltpu.VMEM((value_count, D_K, D_V), F32),
        pltpu.VMEM((value_count, D_K, D_K), BF16),
        pltpu.VMEM((2, n, rows, HEAD_DIM), BF16),
        pltpu.VMEM((q_count, rows, HEAD_DIM), BF16),
        pltpu.VMEM((q_count, rows, 1), F32),
        pltpu.VMEM((q_count, rows, 1), F32),
        pltpu.VMEM((q_count, rows, HEAD_DIM), F32),
        pltpu.VMEM((value_count, D_K, D_V), BF16),
        pltpu.VMEM((value_count, D_K, D_V), BF16),
        like(out_gate),
        like(gate_heads),
        pltpu.SemaphoreType.DMA((18,)),
        pltpu.SemaphoreType.DMA((3,)),
        pltpu.SemaphoreType.DMA((3,)),
        pltpu.SemaphoreType.DMA((n,)),
        pltpu.SemaphoreType.DMA((n,)),
        pltpu.SemaphoreType.DMA((n,)),
        pltpu.SemaphoreType.DMA((n,)),
        pltpu.SemaphoreType.DMA((value_count,)),
        pltpu.SemaphoreType.DMA((value_count,)),
        pltpu.SemaphoreType.DMA((2,)),
    ]
    outs = pl.pallas_call(
        functools.partial(kernel, n),
        out_shape=(
            jax.ShapeDtypeStruct(out_gate.shape, BF16),
            jax.ShapeDtypeStruct(gate_heads.shape, BF16),
        ),
        in_specs=[pl.BlockSpec(memory_space=pl.ANY)] * 18,
        out_specs=(pl.BlockSpec(memory_space=pl.ANY),) * 2,
        scratch_shapes=scratch,
        compiler_params=pltpu.CompilerParams(
            collective_id=0, has_side_effects=True, vmem_limit_bytes=60 * 2**20
        ),
        name="token_mixing",
    )(*ins)
    return pl.pallas_call(
        place,
        out_shape=tuple(jax.ShapeDtypeStruct(a.shape, a.dtype) for a in outs),
        in_specs=[pl.BlockSpec(memory_space=pl.ANY)] * 2,
        out_specs=(pl.BlockSpec(memory_space=pl.ANY),) * 2,
        scratch_shapes=[pltpu.SemaphoreType.DMA((2,))],
        compiler_params=pltpu.CompilerParams(vmem_limit_bytes=60 * 2**20),
        name="place",
    )(*outs)


def solution(mesh):
    tokens = P(("grp", "ctx"), "head")
    taps = P(None, "head")
    shared = P(("grp", "ctx"), None)
    placed = (
        tokens, tokens, tokens, tokens, taps, taps, taps, tokens, tokens, P(),
        tokens, tokens, shared, shared, P(), P(),
    )
    return jax.shard_map(
        body, mesh=mesh, in_specs=placed, out_specs=(tokens, tokens), check_vma=False
    )
```

```python
import functools

import jax
import jax.numpy as jnp
import numpy as np
from jax import lax
from jax.experimental import pallas as pl
from jax.experimental.pallas import tpu as pltpu
from jax.sharding import PartitionSpec as P

D_K = 128
D_V = 128
K_HEADS = 16
VALUE_HEAD_COUNT = 32
CONV = 4
Q_HEADS = 16
KV_HEADS = 2
HEAD_DIM = 256
ROPE_THETA = 10000000.0
REPEATS = VALUE_HEAD_COUNT // K_HEADS
RIM = 16

HIGHEST = lax.Precision.HIGHEST
MESH = pl.DeviceIdType.MESH
F32 = jnp.float32
BF16 = jnp.bfloat16


def mm(left, right):
    return jnp.dot(left.astype(BF16), right.astype(BF16), preferred_element_type=F32)


def mmt(left, right):
    return lax.dot_general(
        left.astype(BF16),
        right.astype(BF16),
        (((1,), (1,)), ((), ())),
        preferred_element_type=F32,
    )


def sigmoid(x):
    return 1.0 / (1.0 + jnp.exp(-x))


def unit_rows(x):
    return x * lax.rsqrt(jnp.sum(x * x, -1, keepdims=True) + 1e-06)


def iotas(rows):
    row = lax.broadcasted_iota(jnp.int32, (rows, rows), 0)
    col = lax.broadcasted_iota(jnp.int32, (rows, rows), 1)
    return row, col


def delta_local(heads, masks):
    lower, strict, eye, same16, same64 = masks
    identity = jnp.where(eye, 1.0, 0.0)
    withins = [
        jnp.where(lower, jnp.exp(jnp.where(lower, h["cum"] - h["cum_row"], 0.0)), 0.0)
        for h in heads
    ]
    couplings = [
        jnp.where(strict, h["beta"] * h["gram"] * within, 0.0)
        for h, within in zip(heads, withins)
    ]
    inners = [(h["scores"] * within).astype(BF16) for h, within in zip(heads, withins)]
    rest16 = [jnp.where(same64 & ~same16, c, 0.0).astype(BF16) for c in couplings]
    rest64 = [jnp.where(same64, 0.0, c).astype(BF16) for c in couplings]

    powers = [jnp.where(same16, -c, 0.0) for c in couplings]
    inverses = [(identity + p).astype(BF16) for p in powers]
    powers = [p.astype(BF16) for p in powers]
    for _ in range(3):
        squares = [mm(p, p) for p in powers]
        factors = [(identity + p).astype(BF16) for p in squares]
        powers = [p.astype(BF16) for p in squares]
        inverses = [mm(i, f).astype(BF16) for i, f in zip(inverses, factors)]

    steps = [-mm(i, r) for i, r in zip(inverses, rest16)]
    seconds = [mm(p, p) for p in steps]
    grows = [
        mm(identity + p, identity + p2).astype(BF16) for p, p2 in zip(steps, seconds)
    ]
    inverses = [mm(g, i).astype(BF16) for g, i in zip(grows, inverses)]

    steps = [(-mm(i, r)).astype(BF16) for i, r in zip(inverses, rest64)]
    seconds = [mm(p, p).astype(BF16) for p in steps]
    decays = [jnp.exp(h["cum"]) for h in heads]
    rights = [
        jnp.concatenate([h["beta"] * h["value"], (h["beta"] * d) * h["key"]], -1)
        for h, d in zip(heads, decays)
    ]
    solved = [mm(i, r) for i, r in zip(inverses, rights)]
    solved = [x + mm(p, x) for x, p in zip(solved, seconds)]
    solved = [(x + mm(p, x)).astype(BF16) for x, p in zip(solved, steps)]

    lasts = [h["cum"][h["cum"].shape[0] - 1 :, :] for h in heads]
    ended = [
        mm(h["key_t"] * jnp.exp(last - h["cum_row"]), x)
        for h, last, x in zip(heads, lasts, solved)
    ]
    boths = [mm(inner, x) for inner, x in zip(inners, solved)]
    krow, kcol = iotas(D_K)
    results = []
    for h, d, last, end, both in zip(heads, decays, lasts, ended, boths):
        transfer = jnp.where(krow == kcol, jnp.exp(last), 0.0) - end[:, D_V:]
        results.append(
            (both[:, :D_V], h["query"] * d - both[:, D_V:], end[:, :D_V], transfer)
        )
    return results


def rope_norm(x, gain, cosine, sine):
    normed = x * lax.rsqrt(jnp.mean(x * x, -1, keepdims=True) + 1e-06) * gain
    half = HEAD_DIM // 8
    front = normed[:, :128]
    lane = lax.broadcasted_iota(jnp.int32, front.shape, 1)
    partner = jnp.where(lane < half, pltpu.roll(front, 128 - half, 1), pltpu.roll(front, half, 1))
    front = front * cosine + partner * sine
    return jnp.concatenate([front, normed[:, 128:]], -1).astype(BF16)


def kernel(n, *refs):
    ins = refs[:18]
    (
        qraw_h, kraw_h, vraw_h, ogate_h, cq_h, ck_h, cv_h, decay_h, beta_h, ngain_h,
        qh_h, gh_h, kh_h, vh_h, qgain_h, kgain_h, cos_h, sin_h,
    ) = ins
    dn_out, at_out = refs[18:20]
    (
        qraw, kraw, vraw, ogate, cq, ck, cv, decay, beta_in, ngain,
        qh, gh, kh, qgain, kgain, cosine, sine,
        rim_q, rim_k, rim_v, pad, cum_s, beta_s, cumt_s,
        out_local_s, state_query_s, offset_s, transfer_s,
        kv, qrot, m_s, l_s, acc_s, in_buf, send_buf, dn_v, at_v,
        load_sem, rim_send, rim_recv, kv_send, kv_recv, pass_send, pass_recv, st_send, st_recv, out_sem,
    ) = refs[20:]
    rows = qraw.shape[0]
    me = lax.axis_index("ctx")
    head = lax.axis_index("head")
    later = jnp.minimum(me + 1, n - 1)
    behind = jnp.maximum(me - 1, 0)
    core = lax.rem(head, 2)
    peer = head + 1 - 2 * core
    key_heads = qraw.shape[1] // D_K
    value_heads = vraw.shape[1] // D_V
    q_heads = qh.shape[1] // HEAD_DIM
    kv_index = head * q_heads // (Q_HEADS // KV_HEADS)
    kv_cols = pl.ds(pl.multiple_of(kv_index * HEAD_DIM, HEAD_DIM), HEAD_DIM)
    own_rows = pl.ds(pl.multiple_of(me * rows, rows), rows)

    barrier = pltpu.get_barrier_semaphore()

    @pl.when(me > 0)
    def _():
        pl.semaphore_signal(barrier, inc=1, device_id={"ctx": behind}, device_id_type=MESH)

    pl.semaphore_signal(barrier, inc=1, device_id={"head": peer}, device_id_type=MESH)

    pairs = [
        (kh_h.at[:, kv_cols], kh),
        (cos_h.at[own_rows], cosine),
        (sin_h.at[own_rows], sine),
        (kgain_h, kgain),
        (vh_h.at[:, kv_cols], kv.at[1, me]),
        (qgain_h, qgain),
        (qh_h, qh),
        (qraw_h, qraw),
        (kraw_h, kraw),
        (vraw_h, vraw),
        (decay_h, decay),
        (beta_h, beta_in),
        (cq_h, cq),
        (ck_h, ck),
        (cv_h, cv),
        (ngain_h, ngain),
        (gh_h, gh),
        (ogate_h, ogate),
    ]
    loads = [
        pltpu.make_async_copy(source, target, load_sem.at[i])
        for i, (source, target) in enumerate(pairs)
    ]
    for load in loads:
        load.start()

    def rim_copy(raw, rim, i, dest):
        return pltpu.make_async_remote_copy(
            src_ref=raw.at[pl.ds(rows - RIM, RIM)],
            dst_ref=rim,
            send_sem=rim_send.at[i],
            recv_sem=rim_recv.at[i],
            device_id={"ctx": dest},
            device_id_type=MESH,
        )

    def kv_copy(block, dest):
        return pltpu.make_async_remote_copy(
            src_ref=kv.at[core, block],
            dst_ref=kv.at[core, block],
            send_sem=kv_send.at[block],
            recv_sem=kv_recv.at[block],
            device_id={"ctx": dest},
            device_id_type=MESH,
        )

    def pass_copy(which, block):
        return pltpu.make_async_remote_copy(
            src_ref=kv.at[which, block],
            dst_ref=kv.at[which, block],
            send_sem=pass_send.at[block],
            recv_sem=pass_recv.at[block],
            device_id={"head": peer},
            device_id_type=MESH,
        )

    def state_copy(h, dest):
        return pltpu.make_async_remote_copy(
            src_ref=send_buf.at[h],
            dst_ref=in_buf.at[h],
            send_sem=st_send.at[h],
            recv_sem=st_recv.at[h],
            device_id={"ctx": dest},
            device_id_type=MESH,
        )

    rims = [(qraw_h, rim_q), (kraw_h, rim_k), (vraw_h, rim_v)]

    pl.semaphore_wait(barrier, 1 + later - me)

    @pl.when(me < n - 1)
    def _():
        for i, (raw, rim) in enumerate(rims):
            rim_copy(raw, rim, i, later).start()

    for load in loads[:5]:
        load.wait()
    kv[0, me] = rope_norm(kh[...].astype(F32), kgain[...], cosine[...], sine[...])

    @pl.when(me < n - 1)
    def _():
        kv_copy(me, later).start()

    for load in loads[5:17]:
        load.wait()

    row, col = iotas(rows)
    ones_low = jnp.where(row >= col, 1.0, 0.0)
    ones_up = jnp.where(row <= col, 1.0, 0.0)
    cumt_s[...] = jnp.dot(decay[...], ones_up, precision=HIGHEST, preferred_element_type=F32)
    cum_s[...] = lax.dot_general(
        ones_low, decay[...], (((1,), (1,)), ((), ())), precision=HIGHEST,
        preferred_element_type=F32,
    )
    beta_s[...] = beta_in[...].T

    @pl.when(me == 0)
    def _():
        for _, rim in rims:
            rim[...] = jnp.zeros_like(rim)
        in_buf[...] = jnp.zeros_like(in_buf)

    scale = HEAD_DIM ** (-0.5)

    def attend(i, block, diagonal):
        scores = mmt(qrot[i], kv[0, block]) * scale
        if diagonal:
            arow, acol = iotas(rows)
            scores = jnp.where(acol <= arow, scores, -1e30)
        top = jnp.max(scores, -1, keepdims=True)
        if diagonal:
            new = top
        else:
            old = m_s[i]
            new = jnp.maximum(old, top)
        expos = jnp.exp(scores - new)
        total = jnp.sum(expos, -1, keepdims=True)
        mixed = mm(expos, kv[1, block])
        if not diagonal:
            factor = jnp.exp(old - new)
            total = total + l_s[i] * factor
            mixed = mixed + acc_s[i] * factor
        m_s[i] = new
        l_s[i] = total
        acc_s[i] = mixed

    def own_block():
        for i in range(q_heads):
            cols = slice(i * HEAD_DIM, (i + 1) * HEAD_DIM)
            qrot[i] = rope_norm(qh[:, cols].astype(F32), qgain[...], cosine[...], sine[...])
            attend(i, me, True)

    @pl.when(me > 0)
    def _():
        own_block()
        for i, (raw, rim) in enumerate(rims):
            rim_copy(raw, rim, i, behind).wait_recv()

    def conv_silu(slot, raw, rim, taps, cols):
        pad[slot, 0:RIM] = rim[:, cols].astype(F32)
        pad[slot, RIM : RIM + rows] = raw[:, cols].astype(F32)
        weights = taps[:, cols]
        total = None
        for j in range(CONV):
            first = RIM - (CONV - 1) + j
            term = weights[j : j + 1] * pad[slot, first : first + rows]
            total = term if total is None else total + term
        return total * sigmoid(total)

    group = 2 if key_heads % 2 == 0 else 1
    groups = key_heads // group

    def ring_step(step):
        block = me - step
        kv_copy(block, behind).wait_recv()
        pass_copy(core, block).start()

        @pl.when(me < n - 1)
        def _():
            kv_copy(block, later).start()

    def head_group(g, carry):
        lane = lax.broadcasted_iota(jnp.int32, (rows, value_heads), 1)
        mrow, mcol = iotas(rows)
        masks = (
            mrow >= mcol, mrow > mcol, mrow == mcol,
            (mrow // 16) == (mcol // 16), (mrow // 64) == (mcol // 64),
        )
        heads = []
        for i in range(group):
            kh_i = g * group + i
            cols = pl.ds(pl.multiple_of(kh_i * D_K, D_K), D_K)
            slot = i * (2 + REPEATS)
            query = unit_rows(conv_silu(slot, qraw, rim_q, cq, cols)) * D_K ** (-0.5)
            key = unit_rows(conv_silu(slot + 1, kraw, rim_k, ck, cols))
            key_t = key.T
            gram = mm(key, key_t)
            scores = mm(query, key_t)
            for r in range(REPEATS):
                h = kh_i * REPEATS + r
                vcols = pl.ds(pl.multiple_of(h * D_V, D_V), D_V)
                heads.append(dict(
                    h=h, vcols=vcols, query=query, key=key, key_t=key_t, gram=gram,
                    scores=scores,
                    value=conv_silu(slot + 2 + r, vraw, rim_v, cv, vcols),
                    cum=jnp.sum(jnp.where(lane == h, cum_s[...], 0.0), -1, keepdims=True),
                    beta=jnp.sum(jnp.where(lane == h, beta_s[...], 0.0), -1, keepdims=True),
                    cum_row=cumt_s[pl.ds(h, 1), :],
                ))
        results = delta_local(heads, masks)
        for item, (out_local, state_query, offset, transfer) in zip(heads, results):
            h, vcols = item["h"], item["vcols"]
            out_local_s[:, vcols] = out_local
            state_query_s[:, vcols] = state_query.astype(BF16)
            offset_s[h] = offset
            transfer_s[h] = transfer.astype(BF16)
            send_buf[h] = offset.astype(BF16)

        @pl.when(me == 0)
        def _():
            for i in range(group * REPEATS):
                state_copy(g * group * REPEATS + i, later).start()

        @pl.when(g + 1 <= me)
        def _():
            ring_step(g + 1)

        return carry

    lax.fori_loop(0, groups, head_group, 0)

    def relay(first, count):
        @pl.loop(first, first + count)
        def _(h):
            state_copy(h, behind).wait_recv()

            @pl.when(me < n - 1)
            def _():
                send_buf[h] = (mm(transfer_s[h], in_buf[h]) + offset_s[h]).astype(BF16)
                state_copy(h, later).start()

    half = value_heads // 2

    @pl.when(me == 0)
    def _():
        own_block()

    @pl.when(me == 1)
    def _():
        relay(0, half)

    @pl.loop(1, me + 1)
    def _(step):
        @pl.when(step > groups)
        def _():
            ring_step(step)

        pass_copy(1 - core, me - step).wait_recv()
        for i in range(q_heads):
            attend(i, me - step, False)

    @pl.when(me > 1)
    def _():
        relay(0, half)

    @pl.when(me > 0)
    def _():
        relay(half, value_heads - half)

    for load in loads[17:]:
        load.wait()

    for i in range(q_heads):
        cols = slice(i * HEAD_DIM, (i + 1) * HEAD_DIM)
        gate = sigmoid(gh[:, cols].astype(F32))
        at_v[:, cols] = (acc_s[i] / l_s[i] * gate).astype(BF16)
    at_copy = pltpu.make_async_copy(at_v, at_out, out_sem.at[0])
    at_copy.start()

    gain = ngain[...]

    @pl.loop(0, value_heads)
    def _(h):
        vcols = pl.ds(pl.multiple_of(h * D_V, D_V), D_V)
        out = out_local_s[:, vcols] + mm(state_query_s[:, vcols], in_buf[h])
        normed = out * lax.rsqrt(jnp.mean(out * out, -1, keepdims=True) + 1e-06) * gain
        gate = ogate[:, vcols].astype(F32)
        dn_v[:, vcols] = (normed * (gate * sigmoid(gate))).astype(BF16)

    dn_copy = pltpu.make_async_copy(dn_v, dn_out, out_sem.at[1])
    dn_copy.start()

    @pl.when(me < n - 1)
    def _():
        for i, (raw, rim) in enumerate(rims):
            rim_copy(raw, rim, i, later).wait_send()

        @pl.loop(0, value_heads)
        def _(h):
            state_copy(h, later).wait_send()

        @pl.loop(0, me + 1)
        def _(block):
            kv_copy(block, later).wait_send()

    @pl.loop(0, me)
    def _(block):
        pass_copy(core, block).wait_send()

    at_copy.wait()
    dn_copy.wait()


def place(first, second, first_out, second_out, held, sem_in, sem_out):
    pieces = held.shape[1]
    rows = held.shape[2]
    arrays = [(first, first_out), (second, second_out)]
    ins, outs = [], []
    for i, (source, target) in enumerate(arrays):
        for j in range(pieces):
            part = pl.ds(j * rows, rows)
            ins.append(
                pltpu.make_async_copy(source.at[part], held.at[i, j], sem_in.at[i, j])
            )
            outs.append(
                pltpu.make_async_copy(held.at[i, j], target.at[part], sem_out.at[i, j])
            )
    for copy in ins:
        copy.start()
    for copy, onward in zip(ins, outs):
        copy.wait()
        onward.start()
    for copy in outs:
        copy.wait()


def rope_tables(count):
    half = HEAD_DIM // 8
    frequency = (ROPE_THETA ** (-np.arange(half, dtype=np.float64) / half)).astype(np.float32)
    angles = np.arange(count, dtype=np.float32)[:, None] * frequency[None, :]
    cosine = np.cos(angles.astype(np.float64)).astype(np.float32)
    sine = np.sin(angles.astype(np.float64)).astype(np.float32)
    one = np.ones((count, 128 - 2 * half), np.float32)
    return (
        np.concatenate([cosine, cosine, one], 1),
        np.concatenate([-sine, sine, 0 * one], 1),
    )


def body(
    query_raw, key_raw, value_raw, out_gate, conv_query, conv_key, conv_value, decay_log,
    write_beta, norm_gain, query_heads, gate_heads, key_heads, value_heads, query_gain, key_gain,
):
    n = lax.axis_size("ctx")
    rows = query_raw.shape[0]
    value_count = value_raw.shape[1] // D_V
    q_count = query_heads.shape[1] // HEAD_DIM
    cosine, sine = rope_tables(n * rows)
    ins = (
        query_raw, key_raw, value_raw, out_gate, conv_query, conv_key, conv_value, decay_log.T,
        write_beta.T, norm_gain[None], query_heads, gate_heads, key_heads, value_heads,
        query_gain[None], key_gain[None], jnp.asarray(cosine), jnp.asarray(sine),
    )
    like = lambda array: pltpu.VMEM(array.shape, array.dtype)
    scratch = [like(a) for a in ins[:12]]
    scratch += [pltpu.VMEM((rows, HEAD_DIM), BF16), like(ins[14]), like(ins[15])]
    scratch += [pltpu.VMEM((rows, 128), F32)] * 2
    scratch += [pltpu.VMEM((RIM, a.shape[1]), BF16) for a in ins[:3]]
    scratch += [
        pltpu.VMEM((2 * (2 + REPEATS), RIM + rows, 128), F32),
        pltpu.VMEM((rows, value_count), F32),
        pltpu.VMEM((rows, value_count), F32),
        pltpu.VMEM((value_count, rows), F32),
        pltpu.VMEM((rows, value_count * D_V), F32),
        pltpu.VMEM((rows, value_count * D_K), BF16),
        pltpu.VMEM((value_count, D_K, D_V), F32),
        pltpu.VMEM((value_count, D_K, D_K), BF16),
        pltpu.VMEM((2, n, rows, HEAD_DIM), BF16),
        pltpu.VMEM((q_count, rows, HEAD_DIM), BF16),
        pltpu.VMEM((q_count, rows, 1), F32),
        pltpu.VMEM((q_count, rows, 1), F32),
        pltpu.VMEM((q_count, rows, HEAD_DIM), F32),
        pltpu.VMEM((value_count, D_K, D_V), BF16),
        pltpu.VMEM((value_count, D_K, D_V), BF16),
        like(out_gate),
        like(gate_heads),
        pltpu.SemaphoreType.DMA((18,)),
        pltpu.SemaphoreType.DMA((3,)),
        pltpu.SemaphoreType.DMA((3,)),
        pltpu.SemaphoreType.DMA((n,)),
        pltpu.SemaphoreType.DMA((n,)),
        pltpu.SemaphoreType.DMA((n,)),
        pltpu.SemaphoreType.DMA((n,)),
        pltpu.SemaphoreType.DMA((value_count,)),
        pltpu.SemaphoreType.DMA((value_count,)),
        pltpu.SemaphoreType.DMA((2,)),
    ]
    outs = pl.pallas_call(
        functools.partial(kernel, n),
        out_shape=(
            jax.ShapeDtypeStruct(out_gate.shape, BF16),
            jax.ShapeDtypeStruct(gate_heads.shape, BF16),
        ),
        in_specs=[pl.BlockSpec(memory_space=pl.ANY)] * 18,
        out_specs=(pl.BlockSpec(memory_space=pl.ANY),) * 2,
        scratch_shapes=scratch,
        compiler_params=pltpu.CompilerParams(
            collective_id=0, has_side_effects=True, vmem_limit_bytes=60 * 2**20
        ),
        name="token_mixing",
    )(*ins)
    return pl.pallas_call(
        place,
        out_shape=tuple(jax.ShapeDtypeStruct(a.shape, a.dtype) for a in outs),
        in_specs=[pl.BlockSpec(memory_space=pl.ANY)] * 2,
        out_specs=(pl.BlockSpec(memory_space=pl.ANY),) * 2,
        scratch_shapes=[
            pltpu.VMEM((2, 4, rows // 4, out_gate.shape[1]), BF16),
            pltpu.SemaphoreType.DMA((2, 4)),
            pltpu.SemaphoreType.DMA((2, 4)),
        ],
        compiler_params=pltpu.CompilerParams(vmem_limit_bytes=60 * 2**20),
        name="place",
    )(*outs)


def solution(mesh):
    tokens = P(("grp", "ctx"), "head")
    taps = P(None, "head")
    shared = P(("grp", "ctx"), None)
    placed = (
        tokens, tokens, tokens, tokens, taps, taps, taps, tokens, tokens, P(),
        tokens, tokens, shared, shared, P(), P(),
    )
    return jax.shard_map(
        body, mesh=mesh, in_specs=placed, out_specs=(tokens, tokens), check_vma=False
    )
```
